32 devices in a mesh: space: 4 (over y, core), date: 8 (over z, x).
Axes of the slice: x: 2, y: 2, z: 4, core: 2. Of those that a mesh axis runs over, the one named last changes fastest.
Arguments:
- obs: bfloat16 [7, 192, 32, 512], P(None, 'date', 'space'), may hold values from -30 to 30
- valid: int32 [192, 32, 512], P('date', 'space'), may hold values from 0 to 1
- days: int32 [192], P('date'), may hold values from 0 to 3649, as said below
Outputs:
- coefficients: float32 [7, 8, 32, 512], P(None, None, 'space', 'date')
- noise_scale: float32 [32, 512], P('space', 'date')
The draws below stay inside these ranges and needn't reach their ends.
Inputs may be any that keep to these rules, and one draw needn't show every extreme that they name: `days`: day numbers of the acquisitions, in no particular order.
All inputs are finite; a program needn't handle non-finite values.
Results may differ from the reference program's by a relative error of at most 0.0003.
Values may be sent and summed in bfloat16 or wider, within the bound.
No kernel may reach another device: no remote copies, remote signals or barrier semaphores. Data moves between devices by JAX's collectives and lax.ppermute only.
A program may use at most 128 MiB of HBM per device.

```python
import math
import jax
import jax.numpy as jnp
import numpy as np
from jax import lax

BANDS = 7
COLS = 512
ITERS = 2
DATES = 192
ROWS = 32


def shared_days(key):
    day_key = jax.random.fold_in(key, 11)
    drawn = jax.random.randint(day_key, (DATES,), 0, 3650, dtype=jnp.int32)
    return drawn.at[0].set(0).at[DATES - 1].set(3649)


def draw_days(key, part):
    return shared_days(key)


def draw_valid(key, part):
    days_now = shared_days(key)
    phase_shift = jax.random.randint(jax.random.fold_in(key, 81), (ROWS, COLS), 0, 365, dtype=jnp.int32)
    cloud_span = jax.random.randint(jax.random.fold_in(key, 91), (ROWS, COLS), 60, 181, dtype=jnp.int32)
    season_day = (days_now[:, None, None] + phase_shift[None]) % 365
    in_cloud = season_day < cloud_span[None]
    clear_odds = jnp.where(in_cloud, 25, 90)
    dice_roll = jax.random.randint(jax.random.fold_in(key, 101), (DATES, ROWS, COLS), 0, 100, dtype=jnp.int32)
    return jnp.where(dice_roll < clear_odds, 1, 0).astype(jnp.int32)


def draw_obs(key, part):
    day_float = shared_days(key).astype(jnp.float32)
    angle = day_float * (2.0 * math.pi / 365.25)
    basis = [jnp.ones_like(day_float), (day_float - 1825.0) / 1825.0]
    for harmonic in range(1, 4):
        basis.append(jnp.cos(harmonic * angle))
        basis.append(jnp.sin(harmonic * angle))
    coef_draw = jnp.clip(jax.random.normal(jax.random.fold_in(key, 21), (BANDS, 8, ROWS, COLS), jnp.float32), -4.0, 4.0) * 0.5
    signal = jnp.zeros((BANDS, DATES, ROWS, COLS), jnp.float32)
    for term in range(8):
        signal = signal + coef_draw[:, term][:, None] * basis[term][None, :, None, None]
    date_scale = jnp.exp(math.log(3.0) * jnp.arange(DATES, dtype=jnp.float32) / (DATES - 1))
    noise_key = jax.random.fold_in(key, 31)
    pixel_key = jax.random.fold_in(key, 41)
    noise = jnp.clip(jax.random.normal(noise_key, (BANDS, DATES, ROWS, COLS), jnp.float32), -6.0, 6.0)
    pixel_scale = jnp.exp(jax.random.uniform(pixel_key, (ROWS, COLS), jnp.float32, math.log(0.5), math.log(2.0)))
    hit_draw = jax.random.uniform(jax.random.fold_in(key, 51), (DATES, ROWS, COLS), jnp.float32)
    size_draw = jax.random.uniform(jax.random.fold_in(key, 61), (DATES, ROWS, COLS), jnp.float32, 8.0, 20.0)
    sign_draw = jax.random.uniform(jax.random.fold_in(key, 71), (DATES, ROWS, COLS), jnp.float32)
    hit_flag = jnp.where(hit_draw < 0.03, 1.0, 0.0)
    sign_flag = jnp.where(sign_draw < 0.7, 1.0, -1.0)
    offset = hit_flag * sign_flag * size_draw
    result = signal + 0.3 * noise * date_scale[None, :, None, None] * pixel_scale[None, None] + offset[None]
    return jnp.clip(result, -30.0, 30.0).astype(jnp.bfloat16)


def setup_inputs(seed: int = 0) -> dict:
    key_list = jax.random.split(jax.random.key(seed), 4)
    return {
        "obs": draw_obs(jax.random.fold_in(key_list[3], 71), 0),
        "valid": draw_valid(jax.random.fold_in(key_list[3], 71), 0),
        "days": draw_days(jax.random.fold_in(key_list[3], 71), 0),
    }


tukey_const = 4.685
ridge_value = 1.0
scale_eps = 1e-06
highest = lax.Precision.HIGHEST
pair_first = np.array([row_index for row_index in range(8) for col_index in range(row_index, 8)], dtype=np.int32)
pair_second = np.array([col_index for row_index in range(8) for col_index in range(row_index, 8)], dtype=np.int32)

def design(day_numbers):
    day_float = day_numbers.astype(jnp.float32)
    columns = [jnp.ones_like(day_float), (day_float - 1825.0) / 1825.0]
    angle = day_float * (2.0 * math.pi / 365.25)
    for harmonic in range(1, 4):
        columns.append(jnp.cos(harmonic * angle))
        columns.append(jnp.sin(harmonic * angle))
    return jnp.stack(columns, axis=1)

def box_sum(padded, row_count, col_count):
    across = padded[0:row_count]
    for offset in range(1, 5):
        across = across + padded[offset:offset + row_count]
    window_sum = across[:, 0:col_count]
    for offset in range(1, 5):
        window_sum = window_sum + across[:, offset:offset + col_count]
    return window_sum

def reference(obs, valid, days):
    design_rows = design(days)
    date_count = design_rows.shape[0]
    pixels = ROWS * COLS
    mask_float = valid.astype(jnp.float32).reshape(date_count, pixels)
    products = design_rows[:, pair_first] * design_rows[:, pair_second]
    counts = box_sum(jnp.pad(jnp.ones((ROWS, COLS), jnp.float32), 2), ROWS, COLS)
    weighted = mask_float
    for step in range(ITERS):
        gram_terms = jnp.dot(products.T.astype(jnp.float32), weighted.astype(jnp.float32), precision=highest, preferred_element_type=jnp.float32)
        crosses = []
        for band in range(BANDS):
            observed = obs[band].astype(jnp.float32).reshape(date_count, pixels)
            crosses.append(jnp.dot(design_rows.T.astype(jnp.float32), (weighted * observed).astype(jnp.float32), precision=highest, preferred_element_type=jnp.float32))
        full_gram = jnp.zeros((8, 8, pixels), jnp.float32)
        full_gram = full_gram.at[pair_first, pair_second].set(gram_terms)
        full_gram = full_gram.at[pair_second, pair_first].set(gram_terms)
        full_gram = full_gram + ridge_value * jnp.eye(8, dtype=jnp.float32)[:, :, None]
        right_sides = jnp.transpose(jnp.stack(crosses, axis=0), (2, 1, 0))
        solved = jnp.linalg.solve(jnp.transpose(full_gram, (2, 0, 1)), right_sides)
        coefficient = jnp.transpose(solved, (2, 1, 0))
        resid_power = jnp.zeros((date_count, pixels), jnp.float32)
        for band in range(BANDS):
            observed = obs[band].astype(jnp.float32).reshape(date_count, pixels)
            misfit = observed - jnp.dot(design_rows.astype(jnp.float32), coefficient[band].astype(jnp.float32), precision=highest, preferred_element_type=jnp.float32)
            resid_power = resid_power + misfit * misfit
        resid_power = resid_power / BANDS
        variance = lax.optimization_barrier(jnp.sum(weighted * resid_power, axis=0)) / (1.0 + gram_terms[0])
        smooth = (box_sum(jnp.pad(variance.reshape(ROWS, COLS), 2), ROWS, COLS) / counts).reshape(pixels)
        if step + 1 < ITERS:
            scaled = jnp.minimum(resid_power / (tukey_const * tukey_const * (smooth[None] + scale_eps)), 1.0)
            weighted = mask_float * (1.0 - scaled) * (1.0 - scaled)
    coefficients = coefficient.reshape(BANDS, 8, ROWS, COLS)
    noise_scale = jnp.sqrt(smooth + scale_eps).reshape(ROWS, COLS)
    return (coefficients, noise_scale)
```

```python
import functools
import math

import jax
import jax.numpy as jnp
import numpy as np
from jax import lax
from jax.experimental import pallas as pl
from jax.experimental.pallas import tpu as pltpu
from jax.sharding import PartitionSpec as P

ITERS = 2
TERMS = 8
LANES = 128
TUKEY = 4.685
RIDGE = 1.0
EPS = 1e-06
VMEM_BYTES = 48 * 1024 * 1024
pairs = [(i, j) for i in range(TERMS) for j in range(i, TERMS)]
pair_first = np.array([i for i, _ in pairs], dtype=np.int32)
pair_second = np.array([j for _, j in pairs], dtype=np.int32)
f32 = jnp.float32
bf16 = jnp.bfloat16


def design(day_numbers):
    day_float = day_numbers.astype(f32)
    columns = [jnp.ones_like(day_float), (day_float - 1825.0) / 1825.0]
    angle = day_float * (2.0 * math.pi / 365.25)
    for harmonic in range(1, 4):
        columns.append(jnp.cos(harmonic * angle))
        columns.append(jnp.sin(harmonic * angle))
    return jnp.stack(columns, axis=1)


def split3(x):
    high = lax.reduce_precision(x, 8, 7)
    rest = x - high
    mid = lax.reduce_precision(rest, 8, 7)
    low = rest - mid
    return high.astype(bf16), mid.astype(bf16), low.astype(bf16)


def split3_kernel(x):
    high = x.astype(bf16)
    rest = x - high.astype(f32)
    mid = rest.astype(bf16)
    low = (rest - mid.astype(f32)).astype(bf16)
    return high, mid, low


def pack_kernel(tiles, date_total, me_ref, obs_ref, valid_ref, *outs):
    me = me_ref[0]
    odd = lax.rem(me, 2) == 1
    bands = obs_ref.shape[0]
    dates = obs_ref.shape[1]
    half = dates // 2
    row = lax.broadcasted_iota(jnp.int32, (half, 8, LANES), 1)
    lane = lax.broadcasted_iota(jnp.int32, (half, 8, LANES), 2)
    top = row < 4
    left = lane < 64
    for place, tile_step in enumerate(tiles):
        tile = lax.div(me, 2) ^ tile_step
        start = pl.multiple_of(tile * LANES, LANES)
        for band in range(bands + 1):
            if band < bands:
                block = obs_ref[band, :, :, pl.ds(start, LANES)].astype(f32)
            else:
                block = valid_ref[:, :, pl.ds(start, LANES)].astype(f32)
            block = block.reshape(half, 2, 8, LANES)
            first, second = block[:, 0], block[:, 1]

            def turned(x):
                down = pltpu.roll(x, 4, 1)
                return down, pltpu.roll(x, 64, 2), pltpu.roll(down, 64, 2)

            down_1, side_1, both_1 = turned(first)
            down_2, side_2, both_2 = turned(second)
            even_block = jnp.where(
                top, jnp.where(left, first, both_1), jnp.where(left, down_2, side_2)
            )
            odd_block = jnp.where(
                top, jnp.where(left, side_1, down_1), jnp.where(left, both_2, second)
            )
            same = jnp.where(odd, odd_block, even_block)
            other = jnp.where(odd, even_block, odd_block)
            rows = dates * 4
            outs[2 * place][band * rows : (band + 1) * rows, :] = same.reshape(rows, LANES).astype(
                bf16
            )
            outs[2 * place + 1][band * rows : (band + 1) * rows, :] = other.reshape(
                rows, LANES
            ).astype(bf16)


def packed_blocks(obs, valid, count, me, width):
    bands, dates, rows, cols = obs.shape
    group = LANES // width
    parts = rows // group
    if width == 64 and rows == 8:
        shape = jax.ShapeDtypeStruct(((bands + 1) * dates * parts, LANES), bf16)
        blocks = [None] * count
        half = count // 4
        for tiles in (tuple(range(half, 2 * half)), tuple(range(half))):
            given = pl.pallas_call(
                functools.partial(pack_kernel, tiles, dates),
                out_shape=[shape] * (2 * len(tiles)),
                in_specs=[
                    pl.BlockSpec(memory_space=pltpu.SMEM),
                    pl.BlockSpec(memory_space=pltpu.VMEM),
                    pl.BlockSpec(memory_space=pltpu.VMEM),
                ],
                out_specs=[pl.BlockSpec(memory_space=pltpu.VMEM)] * (2 * len(tiles)),
                compiler_params=pltpu.CompilerParams(vmem_limit_bytes=VMEM_BYTES),
                name="pack",
            )(me.reshape(1), obs, valid)
            for place, tile_step in enumerate(tiles):
                blocks[2 * tile_step] = given[2 * place]
                blocks[2 * tile_step + 1] = given[2 * place + 1]
        return blocks
    whole = jnp.concatenate([obs, valid.astype(bf16)[None]], axis=0)
    whole = whole.reshape(bands + 1, dates, group, parts, count, width)
    whole = whole.transpose(4, 0, 1, 3, 2, 5)
    whole = whole.reshape(count, (bands + 1) * dates * parts, LANES)
    return [lax.dynamic_index_in_dim(whole, me ^ k, 0, keepdims=False) for k in range(count)]


def solve(gram, cross, bands):
    lower = {}
    scaled = {}
    inverse = []
    for col in range(TERMS):
        pivot = gram[col, col] + RIDGE
        for inner in range(col):
            pivot = pivot - lower[col, inner] * scaled[col, inner]
        inverse.append(1.0 / pivot)
        for row in range(col + 1, TERMS):
            entry = gram[col, row]
            for inner in range(col):
                entry = entry - lower[row, inner] * scaled[col, inner]
            scaled[row, col] = entry
            lower[row, col] = entry * inverse[col]
    beta = {}
    for band in range(bands):
        forward = []
        for row in range(TERMS):
            running = cross[row, band]
            for inner in range(row):
                running = running - lower[row, inner] * forward[inner]
            forward.append(running)
        solved = [None] * TERMS
        for row in reversed(range(TERMS)):
            running = forward[row] * inverse[row]
            for inner in range(row + 1, TERMS):
                running = running - lower[inner, row] * solved[inner]
            solved[row] = running
        for row in range(TERMS):
            beta[row, band] = solved[row]
    return beta


def dot(a, b):
    return jnp.dot(a, b, preferred_element_type=f32)


def add_parts(total, size):
    return sum(total[i * size : (i + 1) * size] for i in range(total.shape[0] // size))


def fit_and_spread(parts, bands, gram_sum, cross_sum, y_ref, weight_of, x_ref, power_ref):
    gram = {ij: gram_sum[n * parts : (n + 1) * parts] for n, ij in enumerate(pairs)}
    cross = {
        (k, b): cross_sum[k * parts : (k + 1) * parts, b * LANES : (b + 1) * LANES]
        for k in range(TERMS)
        for b in range(bands)
    }
    beta = solve(gram, cross, bands)
    flat = jnp.concatenate(
        [jnp.concatenate([beta[k, b] for k in range(TERMS)], axis=0) for b in range(bands)], axis=1
    )
    high, mid, low = split3_kernel(flat)
    right = jnp.concatenate([high, high, high, mid, mid, low], axis=0)
    rows = y_ref.shape[0]
    step = 96
    spread = jnp.zeros((8, LANES), f32)
    for start in range(0, rows, step):
        fitted = dot(x_ref[start : start + step, :], right)
        misfit = y_ref[start : start + step, :].astype(f32) - fitted
        power = jnp.zeros((step, LANES), f32)
        for b in range(bands):
            part = misfit[:, b * LANES : (b + 1) * LANES]
            power = power + part * part
        power = power / bands
        if power_ref is not None:
            power_ref[start : start + step, :] = power
        weighted = weight_of(start, step) * power
        spread = spread + jnp.sum(weighted.reshape(step // 8, 8, LANES), axis=0)
    spread = add_parts(spread, parts)
    return beta, spread / (1.0 + gram[0, 0])


def first_kernel(count, bands, parts, *refs):
    blocks = refs[:count]
    left_ref, gram_left_ref, x_ref = refs[count : count + 3]
    y_ref, mask_ref, power_ref, variance_ref = refs[count + 3 : count + 7]
    product_ref = refs[count + 7]
    rows = blocks[0].shape[0] // (bands + 1)
    for k in range(count):
        mask = blocks[k][bands * rows : (bands + 1) * rows, :]
        mask_ref[k * rows : (k + 1) * rows, :] = mask
        for b in range(bands):
            y = blocks[k][b * rows : (b + 1) * rows, :]
            y_ref[k * rows : (k + 1) * rows, b * LANES : (b + 1) * LANES] = y
            product_ref[k * rows : (k + 1) * rows, b * LANES : (b + 1) * LANES] = y * mask
    cross_sum = add_parts(dot(left_ref[...], product_ref[...]), TERMS * parts)
    gram_sum = add_parts(dot(gram_left_ref[...], mask_ref[...]), len(pairs) * parts)

    def weight_of(start, step):
        return mask_ref[start : start + step, :].astype(f32)

    _, variance = fit_and_spread(
        parts, bands, gram_sum, cross_sum, y_ref, weight_of, x_ref, power_ref
    )
    for place in range(variance_ref.shape[0]):
        variance_ref[place, 0:parts, :] = variance


def smoothed(place_ref, field_ref, parts, width, rows, spaces, count):
    group = LANES // width
    space = place_ref[0]
    me = place_ref[1]

    def rows_of(space_now, date_now):
        block = field_ref[space_now * count + date_now, 0:parts, :]
        return [block if h == 0 else pltpu.roll(block, LANES - h * width, 1) for h in range(group)]

    lane = lax.broadcasted_iota(jnp.int32, (rows, LANES), 1)
    sums = []
    for ds in (-1, 0, 1):
        space_now = jnp.clip(space + ds, 0, spaces - 1)
        row_ok = jnp.where((space + ds >= 0) & (space + ds < spaces), 1.0, 0.0)
        across = jnp.zeros((rows, LANES), f32)
        for dd in (-1, 0, 1):
            date_now = jnp.clip(me + dd, 0, count - 1)
            ok = jnp.where((me + dd >= 0) & (me + dd < count), row_ok, 0.0)
            block = jnp.concatenate(rows_of(space_now, date_now), axis=0)
            block = jnp.where(lane < width, block, 0.0) * ok
            for offset in range(-2, 3):
                shift = dd * width - offset
                if abs(shift) >= width and dd * offset <= 0:
                    continue
                moved = block if shift == 0 else pltpu.roll(block, shift % LANES, 1)
                source = lane + offset - dd * width
                across = across + jnp.where((source >= 0) & (source < width), moved, 0.0)
        sums.append(across)
    tall = jnp.concatenate([sums[0][rows - 2 :], sums[1], sums[2][:2]], axis=0)
    total = tall[0:rows]
    for offset in range(1, 5):
        total = total + tall[offset : offset + rows]
    row_index = lax.broadcasted_iota(jnp.int32, (rows, LANES), 0) + space * rows
    col_index = lane + me * width

    def window(index, whole):
        return (jnp.minimum(index + 2, whole - 1) - jnp.maximum(index - 2, 0) + 1).astype(f32)

    smooth = total / (window(row_index, spaces * rows) * window(col_index, count * width))
    return smooth


def to_lanes(tall, parts, width):
    group = LANES // width
    lane = lax.broadcasted_iota(jnp.int32, (parts, LANES), 1)
    out = tall[0:parts]
    for h in range(1, group):
        moved = pltpu.roll(tall[h * parts : (h + 1) * parts], h * width, 1)
        out = jnp.where(lane >= h * width, moved, out)
    return out


def to_rows(block, width):
    group = LANES // width
    tall = [block if h == 0 else pltpu.roll(block, LANES - h * width, 1) for h in range(group)]
    return jnp.concatenate(tall, axis=0)[:, 0:width]


def second_kernel(shape, *refs):
    bands, parts, width, rows, spaces, count = shape
    place_ref, field_ref, y_ref, mask_ref, power_ref = refs[:5]
    left_ref, gram_left_ref, x_ref = refs[5:8]
    coefficient_ref, variance_ref = refs[8:10]
    weight_ref, w_parts, wy_parts = refs[10], refs[11:14], refs[14:17]
    smooth = smoothed(place_ref, field_ref, parts, width, rows, spaces, count)
    smooth = to_lanes(smooth, parts, width)
    scale = 1.0 / (TUKEY * TUKEY * (smooth + EPS))
    scale = jnp.concatenate([scale] * (8 // parts), axis=0)
    total = y_ref.shape[0]
    step = 96
    for start in range(0, total, step):
        power = power_ref[start : start + step, :].reshape(step // 8, 8, LANES)
        left_over = 1.0 - jnp.minimum(power * scale[None], 1.0)
        mask = mask_ref[start : start + step, :].astype(f32)
        weight = mask * (left_over * left_over).reshape(step, LANES)
        weight_ref[start : start + step, :] = weight
        for ref, part in zip(w_parts, split3_kernel(weight)):
            ref[start : start + step, :] = part
        for b in range(bands):
            y = y_ref[start : start + step, b * LANES : (b + 1) * LANES].astype(f32)
            for ref, part in zip(wy_parts, split3_kernel(weight * y)):
                ref[start : start + step, b * LANES : (b + 1) * LANES] = part

    def moments(a_ref, b_refs, size):
        whole = add_parts(dot(a_ref[...], b_refs[0][...]), size)
        whole = whole + add_parts(dot(a_ref[0 : 2 * size, :], b_refs[1][...]), size)
        return whole + dot(a_ref[0:size, :], b_refs[2][...])

    cross_sum = moments(left_ref, wy_parts, TERMS * parts)
    gram_sum = moments(gram_left_ref, w_parts, len(pairs) * parts)

    def weight_of(start, step):
        return weight_ref[start : start + step, :]

    beta, variance = fit_and_spread(
        parts, bands, gram_sum, cross_sum, y_ref, weight_of, x_ref, None
    )
    for place in range(variance_ref.shape[0]):
        variance_ref[place, 0:parts, :] = variance
    for b in range(bands):
        for k in range(TERMS):
            coefficient_ref[b, k] = to_rows(beta[k, b], width)


def last_kernel(shape, place_ref, field_ref, noise_ref):
    bands, parts, width, rows, spaces, count = shape
    smooth = smoothed(place_ref, field_ref, parts, width, rows, spaces, count)
    noise_ref[...] = jnp.sqrt(smooth[:, 0:width] + EPS)


def on_device(obs, valid, days):
    bands, dates, rows, cols = obs.shape
    count = lax.axis_size("date")
    spaces = lax.axis_size("space")
    me = lax.axis_index("date")
    width = cols // count
    group = LANES // width
    parts = rows // group
    total = count * dates * parts
    shape = (bands, parts, width, rows, spaces, count)
    vmem = pl.BlockSpec(memory_space=pltpu.VMEM)
    smem = pl.BlockSpec(memory_space=pltpu.SMEM)
    params = pltpu.CompilerParams(vmem_limit_bytes=VMEM_BYTES)

    blocks = packed_blocks(obs, valid, count, me, width)
    received = [blocks[0]] + [None] * (count - 1)
    for k in sorted(range(1, count), key=lambda k: (-(k // (count // 2)), k)):
        received[k] = lax.ppermute(blocks[k], "date", [(i, i ^ k) for i in range(count)])

    all_days = lax.all_gather(days, "date", axis=0, tiled=False)
    order = me ^ jnp.arange(count, dtype=jnp.int32)
    x = design(jnp.take(all_days, order, axis=0).reshape(-1))
    same_part = jnp.asarray(np.eye(parts, dtype=np.float32))

    def per_row(columns):
        wide = columns[:, None, :, None] * same_part[None, :, None, :]
        return wide.reshape(total, columns.shape[1] * parts)

    x_parts = [part.astype(f32) for part in split3(x)]
    product_parts = [
        part.astype(f32) for part in split3(x[:, pair_first] * x[:, pair_second])
    ]
    left = jnp.concatenate([per_row(p).T for p in x_parts], axis=0).astype(bf16)
    gram_left = jnp.concatenate([per_row(p).T for p in product_parts], axis=0).astype(bf16)
    high, mid, low = [per_row(p) for p in x_parts]
    x_wide = jnp.concatenate([high, mid, low, high, mid, high], axis=1).astype(bf16)

    place = jnp.stack([lax.axis_index("space"), me]).astype(jnp.int32)
    send = jax.ShapeDtypeStruct((spaces * count, 8, LANES), f32)
    wide = (total, bands * LANES)
    narrow = (total, LANES)
    y, mask, power, variance = pl.pallas_call(
        functools.partial(first_kernel, count, bands, parts),
        out_shape=[
            jax.ShapeDtypeStruct(wide, bf16),
            jax.ShapeDtypeStruct(narrow, bf16),
            jax.ShapeDtypeStruct(narrow, f32),
            send,
        ],
        in_specs=[vmem] * (count + 3),
        out_specs=[vmem] * 4,
        scratch_shapes=[pltpu.VMEM(wide, bf16)],
        compiler_params=params,
        name="first",
    )(*received, left, gram_left, x_wide)
    field = lax.all_to_all(variance, ("space", "date"), 0, 0, tiled=True)
    coefficients, variance = pl.pallas_call(
        functools.partial(second_kernel, shape),
        out_shape=[jax.ShapeDtypeStruct((bands, TERMS, rows, width), f32), send],
        in_specs=[smem] + [vmem] * 7,
        out_specs=[vmem] * 2,
        scratch_shapes=[pltpu.VMEM(narrow, f32)]
        + [pltpu.VMEM(narrow, bf16)] * 3
        + [pltpu.VMEM(wide, bf16)] * 3,
        compiler_params=params,
        name="second",
    )(place, field, y, mask, power, left, gram_left, x_wide)
    field = lax.all_to_all(variance, ("space", "date"), 0, 0, tiled=True)
    noise = pl.pallas_call(
        functools.partial(last_kernel, shape),
        out_shape=jax.ShapeDtypeStruct((rows, width), f32),
        in_specs=[smem, vmem],
        out_specs=vmem,
        compiler_params=params,
        name="last",
    )(place, field)
    return coefficients, noise


def solution(mesh):
    in_specs = (P(None, "date", "space", None), P("date", "space", None), P("date"))
    out_specs = (P(None, None, "space", "date"), P("space", "date"))
    return jax.shard_map(
        on_device, mesh=mesh, in_specs=in_specs, out_specs=out_specs, check_vma=False
    )
```

```python
import functools
import math

import jax
import jax.numpy as jnp
from jax import lax
from jax.experimental import pallas as pl
from jax.experimental.pallas import tpu as pltpu
from jax.sharding import PartitionSpec as P

TERMS = 8
LANES = 128
TUKEY = 4.685
RIDGE = 1.0
EPS = 1e-06
VMEM_BYTES = 16 * 1024 * 1024
INFO_ROWS = 16
pairs = [(i, j) for i in range(TERMS) for j in range(i, TERMS)]
f32 = jnp.float32
bf16 = jnp.bfloat16


def split3_kernel(x):
    high = x.astype(bf16)
    rest = x - high.astype(f32)
    mid = rest.astype(bf16)
    low = (rest - mid.astype(f32)).astype(bf16)
    return high, mid, low


def design_info(day_row, dates):
    row = lax.broadcasted_iota(jnp.int32, (TERMS, LANES), 0)
    lane = lax.broadcasted_iota(jnp.int32, (TERMS, LANES), 1)
    day = jnp.broadcast_to(day_row.astype(f32), (TERMS, LANES))
    angle = (row >> 1).astype(f32) * (day * (2.0 * math.pi / 365.25))
    wave = jnp.where((row & 1) == 0, jnp.cos(angle), jnp.sin(angle))
    x = jnp.where(row == 0, 1.0, jnp.where(row == 1, (day - 1825.0) / 1825.0, wave))
    x = jnp.where(lane < dates, x, 0.0)
    high, mid, low = [part.astype(f32) for part in split3_kernel(x)]
    return jnp.concatenate([high + pltpu.roll(low, 64, 1), mid], axis=0).astype(bf16)


def info_kernel(dates, day_ref, out_ref):
    out_ref[...] = design_info(day_ref[...], dates)


def pack_kernel(tiles, me_ref, day_ref, obs_ref, valid_ref, *outs):
    me = me_ref[0]
    odd = lax.rem(me, 2) == 1
    bands = obs_ref.shape[0]
    dates = obs_ref.shape[1]
    half = dates // 2
    info = design_info(day_ref[...], dates)
    for out in outs:
        out[out.shape[0] - INFO_ROWS :, :] = info
    row = lax.broadcasted_iota(jnp.int32, (half, 8, LANES), 1)
    lane = lax.broadcasted_iota(jnp.int32, (half, 8, LANES), 2)
    top = row < 4
    left = lane < 64
    for place, tile_step in enumerate(tiles):
        tile = lax.div(me, 2) ^ tile_step
        start = pl.multiple_of(tile * LANES, LANES)
        for band in range(bands + 1):
            if band < bands:
                block = obs_ref[band, :, :, pl.ds(start, LANES)].astype(f32)
            else:
                block = valid_ref[:, :, pl.ds(start, LANES)].astype(f32)
            block = block.reshape(half, 2, 8, LANES)
            first, second = block[:, 0], block[:, 1]

            def turned(x):
                down = pltpu.roll(x, 4, 1)
                return down, pltpu.roll(x, 64, 2), pltpu.roll(down, 64, 2)

            down_1, side_1, both_1 = turned(first)
            down_2, side_2, both_2 = turned(second)
            even_block = jnp.where(
                top, jnp.where(left, first, both_1), jnp.where(left, down_2, side_2)
            )
            odd_block = jnp.where(
                top, jnp.where(left, side_1, down_1), jnp.where(left, both_2, second)
            )
            same = jnp.where(odd, odd_block, even_block)
            other = jnp.where(odd, even_block, odd_block)
            rows = dates * 4
            outs[2 * place][band * rows : (band + 1) * rows, :] = same.reshape(rows, LANES).astype(
                bf16
            )
            outs[2 * place + 1][band * rows : (band + 1) * rows, :] = other.reshape(
                rows, LANES
            ).astype(bf16)


def packed_blocks(obs, valid, days, count, me, width):
    bands, dates, rows, cols = obs.shape
    group = LANES // width
    parts = rows // group
    vmem = pl.BlockSpec(memory_space=pltpu.VMEM)
    day_row = jnp.pad(days, (0, LANES - dates)).reshape(1, LANES)
    size = (bands + 1) * dates * parts
    if width == 64 and rows == 8:
        shape = jax.ShapeDtypeStruct((size + INFO_ROWS, LANES), bf16)
        blocks = [None] * count
        half = count // 4
        for tiles in (tuple(range(half, 2 * half)), tuple(range(half))):
            given = pl.pallas_call(
                functools.partial(pack_kernel, tiles),
                out_shape=[shape] * (2 * len(tiles)),
                in_specs=[pl.BlockSpec(memory_space=pltpu.SMEM), vmem, vmem, vmem],
                out_specs=[vmem] * (2 * len(tiles)),
                compiler_params=pltpu.CompilerParams(vmem_limit_bytes=VMEM_BYTES),
                name="pack",
            )(me.reshape(1), day_row, obs, valid)
            for place, tile_step in enumerate(tiles):
                blocks[2 * tile_step] = given[2 * place]
                blocks[2 * tile_step + 1] = given[2 * place + 1]
        return blocks
    info = pl.pallas_call(
        functools.partial(info_kernel, dates),
        out_shape=jax.ShapeDtypeStruct((INFO_ROWS, LANES), bf16),
        in_specs=[vmem],
        out_specs=vmem,
        name="info",
    )(day_row)
    whole = jnp.concatenate([obs, valid.astype(bf16)[None]], axis=0)
    whole = whole.reshape(bands + 1, dates, group, parts, count, width)
    whole = whole.transpose(4, 0, 1, 3, 2, 5)
    whole = whole.reshape(count, size, LANES)
    whole = jnp.concatenate(
        [whole, jnp.broadcast_to(info[None], (count, INFO_ROWS, LANES))], axis=1
    )
    return [lax.dynamic_index_in_dim(whole, me ^ k, 0, keepdims=False) for k in range(count)]


def solve(gram, cross, bands):
    lower = {}
    scaled = {}
    inverse = []
    for col in range(TERMS):
        pivot = gram[col, col] + RIDGE
        for inner in range(col):
            pivot = pivot - lower[col, inner] * scaled[col, inner]
        inverse.append(1.0 / pivot)
        for row in range(col + 1, TERMS):
            entry = gram[col, row]
            for inner in range(col):
                entry = entry - lower[row, inner] * scaled[col, inner]
            scaled[row, col] = entry
            lower[row, col] = entry * inverse[col]
    beta = {}
    for band in range(bands):
        forward = []
        for row in range(TERMS):
            running = cross[row, band]
            for inner in range(row):
                running = running - lower[row, inner] * forward[inner]
            forward.append(running)
        solved = [None] * TERMS
        for row in reversed(range(TERMS)):
            running = forward[row] * inverse[row]
            for inner in range(row + 1, TERMS):
                running = running - lower[inner, row] * solved[inner]
            solved[row] = running
        for row in range(TERMS):
            beta[row, band] = solved[row]
    return beta


def dot(a, b):
    return jnp.dot(a, b, preferred_element_type=f32)


def add_parts(total, size):
    return sum(total[i * size : (i + 1) * size] for i in range(total.shape[0] // size))


def dot_nt(a, b):
    return lax.dot_general(a, b, (((1,), (1,)), ((), ())), preferred_element_type=f32)


def one_hot(shape, first, second):
    row = lax.broadcasted_iota(jnp.int32, shape, 0)
    col = lax.broadcasted_iota(jnp.int32, shape, 1)
    return jnp.where(first(row) == second(col), 1.0, 0.0)


def design_of(infos, dates, parts):
    count = len(infos)
    total = count * dates * parts
    wide = -(-count * dates // LANES) * LANES
    shift = parts.bit_length() - 1
    low_bits = parts - 1
    lane = lax.broadcasted_iota(jnp.int32, (TERMS, LANES), 1)
    sums = [jnp.zeros((TERMS, wide), f32) for _ in range(3)]
    for n, info in enumerate(infos):
        info = info.astype(f32)
        top = info[0:TERMS]
        high = jnp.where(lane < 64, top, 0.0)
        low = jnp.where(lane < 64, pltpu.roll(top, 64, 1), 0.0)
        for c, part in enumerate((high, info[TERMS:], low)):
            if wide > LANES:
                part = jnp.concatenate([part, jnp.zeros((TERMS, wide - LANES), f32)], axis=1)
            if n:
                part = pltpu.roll(part, n * dates, 1)
            sums[c] = sums[c] + part
    x = sums[0] + sums[1] + sums[2]
    stacked = jnp.concatenate(sums + [jnp.zeros((TERMS, wide), f32)], axis=0).astype(bf16)
    spread = one_hot((total, wide), lambda t: t >> shift, lambda d: d).astype(bf16)
    size = TERMS * parts
    repeat = one_hot((3 * size, 4 * TERMS), lambda r: r >> shift, lambda c: c).astype(bf16)
    rows = dot(repeat, stacked)
    same = one_hot((3 * size, total), lambda r: r & low_bits, lambda t: t & low_bits)
    left = (dot_nt(rows.astype(bf16), spread) * same).astype(bf16)
    high, mid, low = rows[0:size], rows[size : 2 * size], rows[2 * size :]
    six = jnp.concatenate([high, mid, low, high, mid, high], axis=0).astype(bf16)
    same = one_hot((total, 6 * size), lambda t: t & low_bits, lambda r: r & low_bits)
    x_wide = (dot_nt(spread, six) * same).astype(bf16)
    products = jnp.concatenate(
        [x[i : i + 1] * x[i:] for i in range(TERMS)] + [jnp.zeros((4, wide), f32)], axis=0
    )
    padded = products.shape[0]
    used = len(pairs) * parts
    product_parts = jnp.concatenate(
        [part.astype(f32) for part in split3_kernel(products)], axis=0
    ).astype(bf16)
    gram_left = []
    same = one_hot((used, total), lambda r: r & low_bits, lambda t: t & low_bits)
    for c in range(3):
        repeat = one_hot((used, 3 * padded), lambda r: (r >> shift) + c * padded, lambda n: n)
        rows = dot(repeat.astype(bf16), product_parts)
        gram_left.append((dot_nt(rows.astype(bf16), spread) * same).astype(bf16))
    return left, gram_left, x_wide


def absorb(blocks, bands, dates, parts, outs, product_ref):
    left_ref, gram_left_ref, x_ref, y_ref, mask_ref = outs
    rows = dates * parts
    left, gram_left, x_wide = design_of(
        [block[(bands + 1) * rows :, :] for block in blocks], dates, parts
    )
    left_ref[...] = left
    x_ref[...] = x_wide
    used = len(pairs) * parts
    for c in range(3):
        gram_left_ref[c * used : (c + 1) * used, :] = gram_left[c]
    for n, block in enumerate(blocks):
        here = slice(n * rows, (n + 1) * rows)
        mask = block[bands * rows : (bands + 1) * rows, :]
        mask_ref[here, :] = mask
        for b in range(bands):
            y = block[b * rows : (b + 1) * rows, :]
            y_ref[here, b * LANES : (b + 1) * LANES] = y
            product_ref[here, b * LANES : (b + 1) * LANES] = y * mask
    cross_sum = add_parts(dot(left_ref[...], product_ref[...]), TERMS * parts)
    gram_sum = add_parts(dot(gram_left_ref[...], mask_ref[...]), used)
    return cross_sum, gram_sum


def absorb_kernel(shape, *refs):
    bands, dates, parts = shape
    blocks, outs, sums, product_ref = refs[:-8], refs[-8:-3], refs[-3:-1], refs[-1]
    cross_sum, gram_sum = absorb(blocks, bands, dates, parts, outs, product_ref)
    sums[0][...] = cross_sum
    sums[1][...] = gram_sum


def fit_and_spread(parts, bands, gram_sum, cross_sum, halves):
    gram = {ij: gram_sum[n * parts : (n + 1) * parts] for n, ij in enumerate(pairs)}
    cross = {
        (k, b): cross_sum[k * parts : (k + 1) * parts, b * LANES : (b + 1) * LANES]
        for k in range(TERMS)
        for b in range(bands)
    }
    beta = solve(gram, cross, bands)
    flat = jnp.concatenate(
        [jnp.concatenate([beta[k, b] for k in range(TERMS)], axis=0) for b in range(bands)], axis=1
    )
    high, mid, low = split3_kernel(flat)
    right = jnp.concatenate([high, high, high, mid, mid, low], axis=0)
    step = 96
    spread = jnp.zeros((8, LANES), f32)
    for y_ref, x_ref, power_ref, weight_of in halves:
        for start in range(0, y_ref.shape[0], step):
            here = slice(start, start + step)
            misfit = y_ref[here, :].astype(f32) - dot(x_ref[here, :], right)
            power = jnp.zeros((step, LANES), f32)
            for b in range(bands):
                part = misfit[:, b * LANES : (b + 1) * LANES]
                power = power + part * part
            power = power / bands
            if power_ref is not None:
                power_ref[here, :] = power
            weighted = weight_of(here) * power
            spread = spread + jnp.sum(weighted.reshape(step // 8, 8, LANES), axis=0)
    spread = add_parts(spread, parts)
    return beta, spread / (1.0 + gram[0, 0])


def first_kernel(shape, half_count, *refs):
    bands, dates, parts = shape
    blocks = refs[:half_count]
    early_x, early_y, early_mask, early_cross, early_gram = refs[half_count : half_count + 5]
    outs = refs[half_count + 5 : half_count + 10]
    early_power, late_power, variance_ref, product_ref = refs[half_count + 10 :]
    cross_sum, gram_sum = absorb(blocks, bands, dates, parts, outs, product_ref)
    _, _, x_ref, y_ref, mask_ref = outs
    halves = [
        (early_y, early_x, early_power, lambda here: early_mask[here, :].astype(f32)),
        (y_ref, x_ref, late_power, lambda here: mask_ref[here, :].astype(f32)),
    ]
    _, variance = fit_and_spread(
        parts, bands, gram_sum + early_gram[...], cross_sum + early_cross[...], halves
    )
    for place in range(variance_ref.shape[0]):
        variance_ref[place] = variance


def smoothed(place_ref, field_ref, parts, width, rows, spaces, count):
    group = LANES // width
    space = place_ref[0]
    me = place_ref[1]

    def rows_of(space_now, date_now):
        block = field_ref[space_now * count + date_now]
        return [block if h == 0 else pltpu.roll(block, LANES - h * width, 1) for h in range(group)]

    lane = lax.broadcasted_iota(jnp.int32, (rows, LANES), 1)
    sums = []
    for ds in (-1, 0, 1):
        space_now = jnp.clip(space + ds, 0, spaces - 1)
        row_ok = jnp.where((space + ds >= 0) & (space + ds < spaces), 1.0, 0.0)
        across = jnp.zeros((rows, LANES), f32)
        for dd in (-1, 0, 1):
            date_now = jnp.clip(me + dd, 0, count - 1)
            ok = jnp.where((me + dd >= 0) & (me + dd < count), row_ok, 0.0)
            block = jnp.concatenate(rows_of(space_now, date_now), axis=0)
            block = jnp.where(lane < width, block, 0.0) * ok
            for offset in range(-2, 3):
                shift = dd * width - offset
                if abs(shift) >= width and dd * offset <= 0:
                    continue
                moved = block if shift == 0 else pltpu.roll(block, shift % LANES, 1)
                source = lane + offset - dd * width
                across = across + jnp.where((source >= 0) & (source < width), moved, 0.0)
        sums.append(across)
    tall = jnp.concatenate([sums[0][rows - 2 :], sums[1], sums[2][:2]], axis=0)
    total = tall[0:rows]
    for offset in range(1, 5):
        total = total + tall[offset : offset + rows]
    row_index = lax.broadcasted_iota(jnp.int32, (rows, LANES), 0) + space * rows
    col_index = lane + me * width

    def window(index, whole):
        return (jnp.minimum(index + 2, whole - 1) - jnp.maximum(index - 2, 0) + 1).astype(f32)

    smooth = total / (window(row_index, spaces * rows) * window(col_index, count * width))
    return smooth


def to_lanes(tall, parts, width):
    group = LANES // width
    lane = lax.broadcasted_iota(jnp.int32, (parts, LANES), 1)
    out = tall[0:parts]
    for h in range(1, group):
        moved = pltpu.roll(tall[h * parts : (h + 1) * parts], h * width, 1)
        out = jnp.where(lane >= h * width, moved, out)
    return out


def to_rows(block, width):
    group = LANES // width
    tall = [block if h == 0 else pltpu.roll(block, LANES - h * width, 1) for h in range(group)]
    return jnp.concatenate(tall, axis=0)[:, 0:width]


def second_kernel(shape, *refs):
    bands, parts, width, rows, spaces, count = shape
    place_ref, field_ref = refs[:2]
    halves = [refs[2:8], refs[8:14]]
    coefficient_ref, variance_ref = refs[14:16]
    weight_ref, w_parts, wy_parts = refs[16], refs[17:20], refs[20:23]
    smooth = smoothed(place_ref, field_ref, parts, width, rows, spaces, count)
    smooth = to_lanes(smooth, parts, width)
    scale = 1.0 / (TUKEY * TUKEY * (smooth + EPS))
    scale = jnp.concatenate([scale] * (8 // parts), axis=0)
    half = halves[0][3].shape[0]
    step = 96
    for n, (_, _, _, y_ref, mask_ref, power_ref) in enumerate(halves):
        for start in range(0, half, step):
            here = slice(start, start + step)
            there = slice(n * half + start, n * half + start + step)
            power = power_ref[here, :].reshape(step // 8, 8, LANES)
            left_over = 1.0 - jnp.minimum(power * scale[None], 1.0)
            mask = mask_ref[here, :].astype(f32)
            weight = mask * (left_over * left_over).reshape(step, LANES)
            weight_ref[there, :] = weight
            for ref, part in zip(w_parts, split3_kernel(weight)):
                ref[there, :] = part
            for b in range(bands):
                y = y_ref[here, b * LANES : (b + 1) * LANES].astype(f32)
                for ref, part in zip(wy_parts, split3_kernel(weight * y)):
                    ref[there, b * LANES : (b + 1) * LANES] = part

    def moments(place, b_refs, size):
        total = 0.0
        for n in range(2):
            a_ref = halves[n][place]
            there = slice(n * half, (n + 1) * half)
            total = total + add_parts(dot(a_ref[...], b_refs[0][there, :]), size)
            total = total + add_parts(dot(a_ref[0 : 2 * size, :], b_refs[1][there, :]), size)
            total = total + dot(a_ref[0:size, :], b_refs[2][there, :])
        return total

    cross_sum = moments(0, wy_parts, TERMS * parts)
    gram_sum = moments(1, w_parts, len(pairs) * parts)
    beta, variance = fit_and_spread(
        parts,
        bands,
        gram_sum,
        cross_sum,
        [
            (halves[0][3], halves[0][2], None, lambda here: weight_ref[here, :]),
            (
                halves[1][3],
                halves[1][2],
                None,
                lambda here: weight_ref[here.start + half : here.stop + half, :],
            ),
        ],
    )
    for place in range(variance_ref.shape[0]):
        variance_ref[place] = variance
    for b in range(bands):
        for k in range(TERMS):
            coefficient_ref[b, k] = to_rows(beta[k, b], width)


def last_kernel(shape, place_ref, field_ref, noise_ref):
    bands, parts, width, rows, spaces, count = shape
    smooth = smoothed(place_ref, field_ref, parts, width, rows, spaces, count)
    noise_ref[...] = jnp.sqrt(smooth[:, 0:width] + EPS)


def on_device(obs, valid, days):
    bands, dates, rows, cols = obs.shape
    count = lax.axis_size("date")
    spaces = lax.axis_size("space")
    me = lax.axis_index("date")
    width = cols // count
    group = LANES // width
    parts = rows // group
    half_count = count // 2
    half = half_count * dates * parts
    shape = (bands, parts, width, rows, spaces, count)
    vmem = pl.BlockSpec(memory_space=pltpu.VMEM)
    smem = pl.BlockSpec(memory_space=pltpu.SMEM)
    params = pltpu.CompilerParams(vmem_limit_bytes=VMEM_BYTES)

    blocks = packed_blocks(obs, valid, days, count, me, width)
    received = [blocks[0]] + [None] * (count - 1)
    for k in range(half_count, count):
        received[k] = lax.ppermute(blocks[k], "date", [(i, i ^ k) for i in range(count)])
    for k in range(1, half_count):
        block = blocks[k]
        if k > 1:
            block, received[k - 1] = lax.optimization_barrier((block, received[k - 1]))
        received[k] = lax.ppermute(block, "date", [(i, i ^ k) for i in range(count)])

    wide = (half, bands * LANES)
    narrow = (half, LANES)
    half_shapes = [
        jax.ShapeDtypeStruct((3 * TERMS * parts, half), bf16),
        jax.ShapeDtypeStruct((3 * len(pairs) * parts, half), bf16),
        jax.ShapeDtypeStruct((half, 6 * TERMS * parts), bf16),
        jax.ShapeDtypeStruct(wide, bf16),
        jax.ShapeDtypeStruct(narrow, bf16),
    ]
    sums = [
        jax.ShapeDtypeStruct((TERMS * parts, bands * LANES), f32),
        jax.ShapeDtypeStruct((len(pairs) * parts, LANES), f32),
    ]
    power = jax.ShapeDtypeStruct(narrow, f32)
    send = jax.ShapeDtypeStruct((spaces * count, parts, LANES), f32)
    *early, early_cross, early_gram = pl.pallas_call(
        functools.partial(absorb_kernel, (bands, dates, parts)),
        out_shape=half_shapes + sums,
        in_specs=[vmem] * half_count,
        out_specs=[vmem] * 7,
        scratch_shapes=[pltpu.VMEM(wide, bf16)],
        compiler_params=params,
        name="absorb",
    )(*received[:half_count])
    *late, early_power, late_power, variance = pl.pallas_call(
        functools.partial(first_kernel, (bands, dates, parts), half_count),
        out_shape=half_shapes + [power, power, send],
        in_specs=[vmem] * (half_count + 5),
        out_specs=[vmem] * 8,
        scratch_shapes=[pltpu.VMEM(wide, bf16)],
        compiler_params=params,
        name="first",
    )(*received[half_count:], early[2], early[3], early[4], early_cross, early_gram)

    place = jnp.stack([lax.axis_index("space"), me]).astype(jnp.int32)
    field = lax.all_to_all(variance, ("space", "date"), 0, 0, tiled=True)
    coefficients, variance = pl.pallas_call(
        functools.partial(second_kernel, shape),
        out_shape=[jax.ShapeDtypeStruct((bands, TERMS, rows, width), f32), send],
        in_specs=[smem] + [vmem] * 13,
        out_specs=[vmem] * 2,
        scratch_shapes=[pltpu.VMEM((2 * half, LANES), f32)]
        + [pltpu.VMEM((2 * half, LANES), bf16)] * 3
        + [pltpu.VMEM((2 * half, bands * LANES), bf16)] * 3,
        compiler_params=params,
        name="second",
    )(place, field, *early, early_power, *late, late_power)
    field = lax.all_to_all(variance, ("space", "date"), 0, 0, tiled=True)
    noise = pl.pallas_call(
        functools.partial(last_kernel, shape),
        out_shape=jax.ShapeDtypeStruct((rows, width), f32),
        in_specs=[smem, vmem],
        out_specs=vmem,
        compiler_params=params,
        name="last",
    )(place, field)
    return coefficients, noise


def solution(mesh):
    in_specs = (P(None, "date", "space", None), P("date", "space", None), P("date"))
    out_specs = (P(None, None, "space", "date"), P("space", "date"))
    return jax.shard_map(
        on_device, mesh=mesh, in_specs=in_specs, out_specs=out_specs, check_vma=False
    )
```

```python
import functools
import math

import jax
import jax.numpy as jnp
from jax import lax
from jax.experimental import pallas as pl
from jax.experimental.pallas import tpu as pltpu
from jax.sharding import PartitionSpec as P

TERMS = 8
LANES = 128
TUKEY = 4.685
RIDGE = 1.0
EPS = 1e-06
VMEM_BYTES = 16 * 1024 * 1024
INFO_ROWS = 16
PACK_VMEM_BYTES = 60 * 1024 * 1024
pairs = [(i, j) for i in range(TERMS) for j in range(i, TERMS)]
f32 = jnp.float32
bf16 = jnp.bfloat16


def split3_kernel(x):
    high = x.astype(bf16)
    rest = x - high.astype(f32)
    mid = rest.astype(bf16)
    low = (rest - mid.astype(f32)).astype(bf16)
    return high, mid, low


def design_info(day_ref, dates):
    row = lax.broadcasted_iota(jnp.int32, (TERMS, LANES), 0)
    lane = lax.broadcasted_iota(jnp.int32, (TERMS, LANES), 1)
    day = jnp.zeros((TERMS, LANES), jnp.int32)
    for n in range(dates):
        day = jnp.where(lane == n, day_ref[n], day)
    day = day.astype(f32)
    angle = (row >> 1).astype(f32) * (day * (2.0 * math.pi / 365.25))
    wave = jnp.where((row & 1) == 0, jnp.cos(angle), jnp.sin(angle))
    x = jnp.where(row == 0, 1.0, jnp.where(row == 1, (day - 1825.0) / 1825.0, wave))
    x = jnp.where(lane < dates, x, 0.0)
    high, mid, low = [part.astype(f32) for part in split3_kernel(x)]
    return jnp.concatenate([high + pltpu.roll(low, 64, 1), mid], axis=0).astype(bf16)


def info_kernel(dates, day_ref, out_ref):
    out_ref[...] = design_info(day_ref, dates)


def pack_kernel(count, day_ref, obs_ref, valid_ref, *refs):
    half = count // 2
    outs = refs[:count]
    obs_here, valid_here, out_here, in_sems, out_sems = refs[count:]
    me = lax.axis_index("date")
    odd = lax.rem(me, 2) == 1
    bands, dates = obs_ref.shape[:2]
    rows = dates * 4
    steps = (*range(half // 2, half), *range(half // 2))
    arrivals = []
    for place, step in enumerate(steps):
        tile = lax.div(me, 2) ^ step
        lanes = pl.ds(pl.multiple_of(tile * LANES, LANES), LANES)
        arrivals.append(
            (
                pltpu.make_async_copy(
                    obs_ref.at[:, :, :, lanes], obs_here.at[place], in_sems.at[2 * place]
                ),
                pltpu.make_async_copy(
                    valid_ref.at[:, :, lanes], valid_here.at[place], in_sems.at[2 * place + 1]
                ),
            )
        )
        for copy in arrivals[place]:
            copy.start()
    info = design_info(day_ref, dates)
    pairs_of_dates = dates // 2
    row = lax.broadcasted_iota(jnp.int32, (pairs_of_dates, 8, LANES), 1)
    lane = lax.broadcasted_iota(jnp.int32, (pairs_of_dates, 8, LANES), 2)
    top = row < 4
    left = lane < 64
    leaving = []
    for place, step in enumerate(steps):
        for copy in arrivals[place]:
            copy.wait()
        for band in range(bands + 1):
            block = (obs_here[place, band] if band < bands else valid_here[place]).astype(f32)
            block = block.reshape(pairs_of_dates, 2, 8, LANES)
            first, second = block[:, 0], block[:, 1]

            def turned(x):
                down = pltpu.roll(x, 4, 1)
                return down, pltpu.roll(x, 64, 2), pltpu.roll(down, 64, 2)

            down_1, side_1, both_1 = turned(first)
            down_2, side_2, both_2 = turned(second)
            even_block = jnp.where(
                top, jnp.where(left, first, both_1), jnp.where(left, down_2, side_2)
            )
            odd_block = jnp.where(
                top, jnp.where(left, side_1, down_1), jnp.where(left, both_2, second)
            )
            same = jnp.where(odd, odd_block, even_block)
            other = jnp.where(odd, even_block, odd_block)
            here = slice(band * rows, (band + 1) * rows)
            out_here[2 * place, here, :] = same.reshape(rows, LANES).astype(bf16)
            out_here[2 * place + 1, here, :] = other.reshape(rows, LANES).astype(bf16)
        for n in (0, 1):
            out_here[2 * place + n, (bands + 1) * rows :, :] = info
            leaving.append(
                pltpu.make_async_copy(
                    out_here.at[2 * place + n], outs[2 * step + n], out_sems.at[2 * place + n]
                )
            )
            leaving[-1].start()
    for copy in leaving:
        copy.wait()


def packed_blocks(obs, valid, days, count, me, width):
    bands, dates, rows, cols = obs.shape
    group = LANES // width
    parts = rows // group
    vmem = pl.BlockSpec(memory_space=pltpu.VMEM)
    smem = pl.BlockSpec(memory_space=pltpu.SMEM)
    size = (bands + 1) * dates * parts
    half = count // 2
    if width == 64 and rows == 8:
        shape = jax.ShapeDtypeStruct((size + INFO_ROWS, LANES), bf16)
        hbm = pl.BlockSpec(memory_space=pltpu.HBM)
        return pl.pallas_call(
            functools.partial(pack_kernel, count),
            out_shape=[shape] * count,
            in_specs=[smem, hbm, hbm],
            out_specs=[hbm] * count,
            scratch_shapes=[
                pltpu.VMEM((half, bands, dates, rows, LANES), bf16),
                pltpu.VMEM((half, dates, rows, LANES), jnp.int32),
                pltpu.VMEM((count, size + INFO_ROWS, LANES), bf16),
                pltpu.SemaphoreType.DMA((count,)),
                pltpu.SemaphoreType.DMA((count,)),
            ],
            compiler_params=pltpu.CompilerParams(vmem_limit_bytes=PACK_VMEM_BYTES),
            name="pack",
        )(days, obs, valid)
    info = pl.pallas_call(
        functools.partial(info_kernel, dates),
        out_shape=jax.ShapeDtypeStruct((INFO_ROWS, LANES), bf16),
        in_specs=[smem],
        out_specs=vmem,
        name="info",
    )(days)
    whole = jnp.concatenate([obs, valid.astype(bf16)[None]], axis=0)
    whole = whole.reshape(bands + 1, dates, group, parts, count, width)
    whole = whole.transpose(4, 0, 1, 3, 2, 5)
    whole = whole.reshape(count, size, LANES)
    whole = jnp.concatenate(
        [whole, jnp.broadcast_to(info[None], (count, INFO_ROWS, LANES))], axis=1
    )
    return [lax.dynamic_index_in_dim(whole, me ^ k, 0, keepdims=False) for k in range(count)]


def solve(gram, cross, bands):
    lower = {}
    scaled = {}
    inverse = []
    for col in range(TERMS):
        pivot = gram[col, col] + RIDGE
        for inner in range(col):
            pivot = pivot - lower[col, inner] * scaled[col, inner]
        inverse.append(1.0 / pivot)
        for row in range(col + 1, TERMS):
            entry = gram[col, row]
            for inner in range(col):
                entry = entry - lower[row, inner] * scaled[col, inner]
            scaled[row, col] = entry
            lower[row, col] = entry * inverse[col]
    beta = {}
    for band in range(bands):
        forward = []
        for row in range(TERMS):
            running = cross[row, band]
            for inner in range(row):
                running = running - lower[row, inner] * forward[inner]
            forward.append(running)
        solved = [None] * TERMS
        for row in reversed(range(TERMS)):
            running = forward[row] * inverse[row]
            for inner in range(row + 1, TERMS):
                running = running - lower[inner, row] * solved[inner]
            solved[row] = running
        for row in range(TERMS):
            beta[row, band] = solved[row]
    return beta


def dot(a, b):
    return jnp.dot(a, b, preferred_element_type=f32)


def add_parts(total, size):
    return sum(total[i * size : (i + 1) * size] for i in range(total.shape[0] // size))


def dot_nt(a, b):
    return lax.dot_general(a, b, (((1,), (1,)), ((), ())), preferred_element_type=f32)


def one_hot(shape, first, second):
    row = lax.broadcasted_iota(jnp.int32, shape, 0)
    col = lax.broadcasted_iota(jnp.int32, shape, 1)
    return jnp.where(first(row) == second(col), 1.0, 0.0)


def design_of(infos, dates, parts):
    count = len(infos)
    total = count * dates * parts
    wide = -(-count * dates // LANES) * LANES
    shift = parts.bit_length() - 1
    low_bits = parts - 1
    lane = lax.broadcasted_iota(jnp.int32, (TERMS, LANES), 1)
    sums = [jnp.zeros((TERMS, wide), f32) for _ in range(3)]
    for n, info in enumerate(infos):
        info = info.astype(f32)
        top = info[0:TERMS]
        high = jnp.where(lane < 64, top, 0.0)
        low = jnp.where(lane < 64, pltpu.roll(top, 64, 1), 0.0)
        for c, part in enumerate((high, info[TERMS:], low)):
            if wide > LANES:
                part = jnp.concatenate([part, jnp.zeros((TERMS, wide - LANES), f32)], axis=1)
            if n:
                part = pltpu.roll(part, n * dates, 1)
            sums[c] = sums[c] + part
    x = sums[0] + sums[1] + sums[2]
    stacked = jnp.concatenate(sums + [jnp.zeros((TERMS, wide), f32)], axis=0).astype(bf16)
    spread = one_hot((total, wide), lambda t: t >> shift, lambda d: d).astype(bf16)
    size = TERMS * parts
    repeat = one_hot((3 * size, 4 * TERMS), lambda r: r >> shift, lambda c: c).astype(bf16)
    rows = dot(repeat, stacked)
    same = one_hot((3 * size, total), lambda r: r & low_bits, lambda t: t & low_bits)
    left = (dot_nt(rows.astype(bf16), spread) * same).astype(bf16)
    high, mid, low = rows[0:size], rows[size : 2 * size], rows[2 * size :]
    six = jnp.concatenate([high, mid, low, high, mid, high], axis=0).astype(bf16)
    same = one_hot((total, 6 * size), lambda t: t & low_bits, lambda r: r & low_bits)
    x_wide = (dot_nt(spread, six) * same).astype(bf16)
    products = jnp.concatenate(
        [x[i : i + 1] * x[i:] for i in range(TERMS)] + [jnp.zeros((4, wide), f32)], axis=0
    )
    padded = products.shape[0]
    used = len(pairs) * parts
    product_parts = jnp.concatenate(
        [part.astype(f32) for part in split3_kernel(products)], axis=0
    ).astype(bf16)
    gram_left = []
    same = one_hot((used, total), lambda r: r & low_bits, lambda t: t & low_bits)
    for c in range(3):
        repeat = one_hot((used, 3 * padded), lambda r: (r >> shift) + c * padded, lambda n: n)
        rows = dot(repeat.astype(bf16), product_parts)
        gram_left.append((dot_nt(rows.astype(bf16), spread) * same).astype(bf16))
    return left, gram_left, x_wide


def absorb(blocks, bands, dates, parts, outs, product_ref):
    left_ref, gram_left_ref, x_ref, y_ref, mask_ref = outs
    rows = dates * parts
    left, gram_left, x_wide = design_of(
        [block[(bands + 1) * rows :, :] for block in blocks], dates, parts
    )
    left_ref[...] = left
    x_ref[...] = x_wide
    used = len(pairs) * parts
    for c in range(3):
        gram_left_ref[c * used : (c + 1) * used, :] = gram_left[c]
    for n, block in enumerate(blocks):
        here = slice(n * rows, (n + 1) * rows)
        mask = block[bands * rows : (bands + 1) * rows, :]
        mask_ref[here, :] = mask
        for b in range(bands):
            y = block[b * rows : (b + 1) * rows, :]
            y_ref[here, b * LANES : (b + 1) * LANES] = y
            product_ref[here, b * LANES : (b + 1) * LANES] = y * mask
    cross_sum = add_parts(dot(left_ref[...], product_ref[...]), TERMS * parts)
    gram_sum = add_parts(dot(gram_left_ref[...], mask_ref[...]), used)
    return cross_sum, gram_sum


def single_blocks(refs):
    blocks = []
    for ref in refs:
        blocks += [ref] if len(ref.shape) == 2 else [ref.at[n] for n in range(ref.shape[0])]
    return blocks


def absorb_kernel(shape, *refs):
    bands, dates, parts = shape
    outs, sums, product_ref = refs[-8:-3], refs[-3:-1], refs[-1]
    blocks = single_blocks(refs[:-8])
    cross_sum, gram_sum = absorb(blocks, bands, dates, parts, outs, product_ref)
    sums[0][...] = cross_sum
    sums[1][...] = gram_sum


def fit_and_spread(parts, bands, gram_sum, cross_sum, groups):
    gram = {ij: gram_sum[n * parts : (n + 1) * parts] for n, ij in enumerate(pairs)}
    cross = {
        (k, b): cross_sum[k * parts : (k + 1) * parts, b * LANES : (b + 1) * LANES]
        for k in range(TERMS)
        for b in range(bands)
    }
    beta = solve(gram, cross, bands)
    flat = jnp.concatenate(
        [jnp.concatenate([beta[k, b] for k in range(TERMS)], axis=0) for b in range(bands)], axis=1
    )
    high, mid, low = split3_kernel(flat)
    right = jnp.concatenate([high, high, high, mid, mid, low], axis=0)
    step = 96
    spread = jnp.zeros((8, LANES), f32)
    for y_ref, x_ref, power_ref, weight_of in groups:
        for start in range(0, y_ref.shape[0], step):
            here = slice(start, start + step)
            misfit = y_ref[here, :].astype(f32) - dot(x_ref[here, :], right)
            power = jnp.zeros((step, LANES), f32)
            for b in range(bands):
                part = misfit[:, b * LANES : (b + 1) * LANES]
                power = power + part * part
            power = power / bands
            if power_ref is not None:
                power_ref[here, :] = power
            weighted = weight_of(here) * power
            spread = spread + jnp.sum(weighted.reshape(step // 8, 8, LANES), axis=0)
    spread = add_parts(spread, parts)
    return beta, spread / (1.0 + gram[0, 0])


def first_kernel(shape, arrays, *refs):
    bands, dates, parts = shape
    blocks = single_blocks(refs[:arrays])
    early_x, early_y, early_mask, early_cross, early_gram = refs[arrays : arrays + 5]
    outs = refs[arrays + 5 : arrays + 10]
    early_power, late_power, variance_ref, product_ref = refs[arrays + 10 :]
    cross_sum, gram_sum = absorb(blocks, bands, dates, parts, outs, product_ref)
    _, _, x_ref, y_ref, mask_ref = outs
    groups = [
        (early_y, early_x, early_power, lambda here: early_mask[here, :].astype(f32)),
        (y_ref, x_ref, late_power, lambda here: mask_ref[here, :].astype(f32)),
    ]
    _, variance = fit_and_spread(
        parts, bands, gram_sum + early_gram[...], cross_sum + early_cross[...], groups
    )
    for place in range(variance_ref.shape[0]):
        variance_ref[place] = variance


def smoothed(field_ref, parts, width, rows, spaces, count):
    group = LANES // width
    space = lax.axis_index("space")
    me = lax.axis_index("date")

    def rows_of(space_now, date_now):
        block = field_ref[space_now * count + date_now]
        return [block if h == 0 else pltpu.roll(block, LANES - h * width, 1) for h in range(group)]

    lane = lax.broadcasted_iota(jnp.int32, (rows, LANES), 1)
    sums = []
    for ds in (-1, 0, 1):
        space_now = jnp.clip(space + ds, 0, spaces - 1)
        row_ok = jnp.where((space + ds >= 0) & (space + ds < spaces), 1.0, 0.0)
        across = jnp.zeros((rows, LANES), f32)
        for dd in (-1, 0, 1):
            date_now = jnp.clip(me + dd, 0, count - 1)
            ok = jnp.where((me + dd >= 0) & (me + dd < count), row_ok, 0.0)
            block = jnp.concatenate(rows_of(space_now, date_now), axis=0)
            block = jnp.where(lane < width, block, 0.0) * ok
            for offset in range(-2, 3):
                shift = dd * width - offset
                if abs(shift) >= width and dd * offset <= 0:
                    continue
                moved = block if shift == 0 else pltpu.roll(block, shift % LANES, 1)
                source = lane + offset - dd * width
                across = across + jnp.where((source >= 0) & (source < width), moved, 0.0)
        sums.append(across)
    tall = jnp.concatenate([sums[0][rows - 2 :], sums[1], sums[2][:2]], axis=0)
    total = tall[0:rows]
    for offset in range(1, 5):
        total = total + tall[offset : offset + rows]
    row_index = lax.broadcasted_iota(jnp.int32, (rows, LANES), 0) + space * rows
    col_index = lane + me * width

    def window(index, whole):
        return (jnp.minimum(index + 2, whole - 1) - jnp.maximum(index - 2, 0) + 1).astype(f32)

    smooth = total / (window(row_index, spaces * rows) * window(col_index, count * width))
    return smooth


def to_lanes(tall, parts, width):
    group = LANES // width
    lane = lax.broadcasted_iota(jnp.int32, (parts, LANES), 1)
    out = tall[0:parts]
    for h in range(1, group):
        moved = pltpu.roll(tall[h * parts : (h + 1) * parts], h * width, 1)
        out = jnp.where(lane >= h * width, moved, out)
    return out


def to_rows(block, width):
    group = LANES // width
    tall = [block if h == 0 else pltpu.roll(block, LANES - h * width, 1) for h in range(group)]
    return jnp.concatenate(tall, axis=0)[:, 0:width]


def second_kernel(shape, *refs):
    bands, parts, width, rows, spaces, count = shape
    field_ref = refs[0]
    groups = [refs[1:7], refs[7:13]]
    coefficient_ref, variance_ref = refs[13:15]
    weight_ref, w_parts, wy_parts = refs[15], refs[16:19], refs[19:22]
    smooth = smoothed(field_ref, parts, width, rows, spaces, count)
    smooth = to_lanes(smooth, parts, width)
    scale = 1.0 / (TUKEY * TUKEY * (smooth + EPS))
    scale = jnp.concatenate([scale] * (8 // parts), axis=0)
    early = groups[0][3].shape[0]
    step = 96
    for base, (_, _, _, y_ref, mask_ref, power_ref) in zip((0, early), groups):
        for start in range(0, y_ref.shape[0], step):
            here = slice(start, start + step)
            there = slice(base + start, base + start + step)
            power = power_ref[here, :].reshape(step // 8, 8, LANES)
            left_over = 1.0 - jnp.minimum(power * scale[None], 1.0)
            mask = mask_ref[here, :].astype(f32)
            weight = mask * (left_over * left_over).reshape(step, LANES)
            weight_ref[there, :] = weight
            for ref, part in zip(w_parts, split3_kernel(weight)):
                ref[there, :] = part
            for b in range(bands):
                y = y_ref[here, b * LANES : (b + 1) * LANES].astype(f32)
                for ref, part in zip(wy_parts, split3_kernel(weight * y)):
                    ref[there, b * LANES : (b + 1) * LANES] = part

    def moments(place, b_refs, size):
        total = 0.0
        for base, group in zip((0, early), groups):
            a_ref = group[place]
            there = slice(base, base + group[3].shape[0])
            total = total + add_parts(dot(a_ref[...], b_refs[0][there, :]), size)
            total = total + add_parts(dot(a_ref[0 : 2 * size, :], b_refs[1][there, :]), size)
            total = total + dot(a_ref[0:size, :], b_refs[2][there, :])
        return total

    cross_sum = moments(0, wy_parts, TERMS * parts)
    gram_sum = moments(1, w_parts, len(pairs) * parts)
    beta, variance = fit_and_spread(
        parts,
        bands,
        gram_sum,
        cross_sum,
        [
            (groups[0][3], groups[0][2], None, lambda here: weight_ref[here, :]),
            (
                groups[1][3],
                groups[1][2],
                None,
                lambda here: weight_ref[here.start + early : here.stop + early, :],
            ),
        ],
    )
    for place in range(variance_ref.shape[0]):
        variance_ref[place] = variance
    for b in range(bands):
        for k in range(TERMS):
            coefficient_ref[b, k] = to_rows(beta[k, b], width)


def last_kernel(shape, field_ref, noise_ref):
    bands, parts, width, rows, spaces, count = shape
    smooth = smoothed(field_ref, parts, width, rows, spaces, count)
    noise_ref[...] = jnp.sqrt(smooth[:, 0:width] + EPS)


def on_device(obs, valid, days):
    bands, dates, rows, cols = obs.shape
    count = lax.axis_size("date")
    spaces = lax.axis_size("space")
    me = lax.axis_index("date")
    width = cols // count
    group = LANES // width
    parts = rows // group
    half = count // 2
    quarter = half // 2
    early_count, late_count = half + quarter, quarter
    early_rows = early_count * dates * parts
    late_rows = late_count * dates * parts
    shape = (bands, parts, width, rows, spaces, count)
    vmem = pl.BlockSpec(memory_space=pltpu.VMEM)
    params = pltpu.CompilerParams(vmem_limit_bytes=VMEM_BYTES)

    blocks = packed_blocks(obs, valid, days, count, me, width)
    received = [blocks[0]] + [None] * (count - 1)

    def swap(k, after=None):
        block = blocks[k]
        if after is not None:
            block, received[after] = lax.optimization_barrier((block, received[after]))
        received[k] = lax.ppermute(block, "date", [(i, i ^ k) for i in range(count)])

    for k in range(half, count, 2):
        swap(k)
    for k in range(1, half):
        swap(k)
    for k in range(half + 1, count, 2):
        swap(k, after=k - 1)
    early_blocks = [*received[:half], *received[half::2]]
    late_blocks = received[half + 1 :: 2]

    def group_shapes(total):
        return [
            jax.ShapeDtypeStruct((3 * TERMS * parts, total), bf16),
            jax.ShapeDtypeStruct((3 * len(pairs) * parts, total), bf16),
            jax.ShapeDtypeStruct((total, 6 * TERMS * parts), bf16),
            jax.ShapeDtypeStruct((total, bands * LANES), bf16),
            jax.ShapeDtypeStruct((total, LANES), bf16),
        ]

    def power(total):
        return jax.ShapeDtypeStruct((total, LANES), f32)

    sums = [
        jax.ShapeDtypeStruct((TERMS * parts, bands * LANES), f32),
        jax.ShapeDtypeStruct((len(pairs) * parts, LANES), f32),
    ]
    send = jax.ShapeDtypeStruct((spaces * count, parts, LANES), f32)
    *early, early_cross, early_gram = pl.pallas_call(
        functools.partial(absorb_kernel, (bands, dates, parts)),
        out_shape=group_shapes(early_rows) + sums,
        in_specs=[vmem] * len(early_blocks),
        out_specs=[vmem] * 7,
        scratch_shapes=[pltpu.VMEM((early_rows, bands * LANES), bf16)],
        compiler_params=params,
        name="absorb",
    )(*early_blocks)
    *late, early_power, late_power, variance = pl.pallas_call(
        functools.partial(first_kernel, (bands, dates, parts), len(late_blocks)),
        out_shape=group_shapes(late_rows) + [power(early_rows), power(late_rows), send],
        in_specs=[vmem] * (len(late_blocks) + 5),
        out_specs=[vmem] * 8,
        scratch_shapes=[pltpu.VMEM((late_rows, bands * LANES), bf16)],
        compiler_params=params,
        name="first",
    )(*late_blocks, early[2], early[3], early[4], early_cross, early_gram)

    field = lax.all_to_all(variance, ("space", "date"), 0, 0, tiled=True)
    total = early_rows + late_rows
    coefficients, variance = pl.pallas_call(
        functools.partial(second_kernel, shape),
        out_shape=[jax.ShapeDtypeStruct((bands, TERMS, rows, width), f32), send],
        in_specs=[vmem] * 13,
        out_specs=[vmem] * 2,
        scratch_shapes=[pltpu.VMEM((total, LANES), f32)]
        + [pltpu.VMEM((total, LANES), bf16)] * 3
        + [pltpu.VMEM((total, bands * LANES), bf16)] * 3,
        compiler_params=params,
        name="second",
    )(field, *early, early_power, *late, late_power)
    field = lax.all_to_all(variance, ("space", "date"), 0, 0, tiled=True)
    noise = pl.pallas_call(
        functools.partial(last_kernel, shape),
        out_shape=jax.ShapeDtypeStruct((rows, width), f32),
        in_specs=[vmem],
        out_specs=vmem,
        compiler_params=params,
        name="last",
    )(field)
    return coefficients, noise


def solution(mesh):
    in_specs = (P(None, "date", "space", None), P("date", "space", None), P("date"))
    out_specs = (P(None, None, "space", "date"), P("space", "date"))
    return jax.shard_map(
        on_device, mesh=mesh, in_specs=in_specs, out_specs=out_specs, check_vma=False
    )
```

```python
import functools
import math

import jax
import jax.numpy as jnp
from jax import lax
from jax.experimental import pallas as pl
from jax.experimental.pallas import tpu as pltpu
from jax.sharding import PartitionSpec as P

TERMS = 8
LANES = 128
TUKEY = 4.685
RIDGE = 1.0
EPS = 1e-06
VMEM_BYTES = 16 * 1024 * 1024
INFO_ROWS = 16
PACK_VMEM_BYTES = 60 * 1024 * 1024
pairs = [(i, j) for i in range(TERMS) for j in range(i, TERMS)]
f32 = jnp.float32
bf16 = jnp.bfloat16


def split2_kernel(x):
    high = x.astype(bf16)
    return high, (x - high.astype(f32)).astype(bf16)


def split3_kernel(x):
    high = x.astype(bf16)
    rest = x - high.astype(f32)
    mid = rest.astype(bf16)
    low = (rest - mid.astype(f32)).astype(bf16)
    return high, mid, low


def design_info(day_ref, dates):
    row = lax.broadcasted_iota(jnp.int32, (TERMS, LANES), 0)
    lane = lax.broadcasted_iota(jnp.int32, (TERMS, LANES), 1)
    day = jnp.zeros((TERMS, LANES), jnp.int32)
    for n in range(dates):
        day = jnp.where(lane == n, day_ref[n], day)
    day = day.astype(f32)
    angle = (row >> 1).astype(f32) * (day * (2.0 * math.pi / 365.25))
    wave = jnp.where((row & 1) == 0, jnp.cos(angle), jnp.sin(angle))
    x = jnp.where(row == 0, 1.0, jnp.where(row == 1, (day - 1825.0) / 1825.0, wave))
    x = jnp.where(lane < dates, x, 0.0)
    high, mid, low = [part.astype(f32) for part in split3_kernel(x)]
    return jnp.concatenate([high + pltpu.roll(low, 64, 1), mid], axis=0).astype(bf16)


def info_kernel(dates, day_ref, out_ref):
    out_ref[...] = design_info(day_ref, dates)


def pack_kernel(steps, day_ref, obs_ref, valid_ref, *refs):
    outs = refs[: 2 * len(steps)]
    day_here, obs_here, valid_here, sems, day_sem = refs[2 * len(steps) :]
    me = lax.axis_index("date")
    odd = lax.rem(me, 2) == 1
    bands, dates = obs_ref.shape[:2]
    rows = dates * 4
    day_copy = pltpu.make_async_copy(day_ref, day_here, day_sem)
    day_copy.start()
    arrivals = []
    for place, step in enumerate(steps):
        tile = lax.div(me, 2) ^ step
        lanes = pl.ds(pl.multiple_of(tile * LANES, LANES), LANES)
        arrivals.append(
            (
                pltpu.make_async_copy(
                    obs_ref.at[:, :, :, lanes], obs_here.at[place], sems.at[2 * place]
                ),
                pltpu.make_async_copy(
                    valid_ref.at[:, :, lanes], valid_here.at[place], sems.at[2 * place + 1]
                ),
            )
        )
        for copy in arrivals[place]:
            copy.start()
    day_copy.wait()
    info = design_info(day_here, dates)
    pairs_of_dates = dates // 2
    row = lax.broadcasted_iota(jnp.int32, (pairs_of_dates, 8, LANES), 1)
    lane = lax.broadcasted_iota(jnp.int32, (pairs_of_dates, 8, LANES), 2)
    top = row < 4
    left = lane < 64
    for place, step in enumerate(steps):
        for copy in arrivals[place]:
            copy.wait()
        for band in range(bands + 1):
            block = (obs_here[place, band] if band < bands else valid_here[place]).astype(f32)
            block = block.reshape(pairs_of_dates, 2, 8, LANES)
            first, second = block[:, 0], block[:, 1]

            def turned(x):
                down = pltpu.roll(x, 4, 1)
                return down, pltpu.roll(x, 64, 2), pltpu.roll(down, 64, 2)

            down_1, side_1, both_1 = turned(first)
            down_2, side_2, both_2 = turned(second)
            even_block = jnp.where(
                top, jnp.where(left, first, both_1), jnp.where(left, down_2, side_2)
            )
            odd_block = jnp.where(
                top, jnp.where(left, side_1, down_1), jnp.where(left, both_2, second)
            )
            same = jnp.where(odd, odd_block, even_block)
            other = jnp.where(odd, even_block, odd_block)
            here = slice(band * rows, (band + 1) * rows)
            outs[2 * place][here, :] = same.reshape(rows, LANES).astype(bf16)
            outs[2 * place + 1][here, :] = other.reshape(rows, LANES).astype(bf16)
        for n in (0, 1):
            outs[2 * place + n][(bands + 1) * rows :, :] = info


def packed_blocks(obs, valid, days, count, me, width):
    bands, dates, rows, cols = obs.shape
    group = LANES // width
    parts = rows // group
    vmem = pl.BlockSpec(memory_space=pltpu.VMEM)
    smem = pl.BlockSpec(memory_space=pltpu.SMEM)
    size = (bands + 1) * dates * parts
    half = count // 2
    if width == 64 and rows == 8:
        hbm = pl.BlockSpec(memory_space=pltpu.HBM)
        blocks = [None] * count
        for steps in (range(half // 2, half), range(half // 2)):
            tiles = len(steps)
            blocks[2 * steps[0] : 2 * steps[-1] + 2] = pl.pallas_call(
                functools.partial(pack_kernel, tuple(steps)),
                out_shape=[jax.ShapeDtypeStruct((size + INFO_ROWS, LANES), bf16)] * (2 * tiles),
                in_specs=[hbm] * 3,
                out_specs=[vmem] * (2 * tiles),
                scratch_shapes=[
                    pltpu.SMEM((dates,), jnp.int32),
                    pltpu.VMEM((tiles, bands, dates, rows, LANES), bf16),
                    pltpu.VMEM((tiles, dates, rows, LANES), jnp.int32),
                    pltpu.SemaphoreType.DMA((2 * tiles,)),
                    pltpu.SemaphoreType.DMA,
                ],
                compiler_params=pltpu.CompilerParams(vmem_limit_bytes=PACK_VMEM_BYTES),
                name="pack",
            )(days, obs, valid)
        return blocks
    info = pl.pallas_call(
        functools.partial(info_kernel, dates),
        out_shape=jax.ShapeDtypeStruct((INFO_ROWS, LANES), bf16),
        in_specs=[smem],
        out_specs=vmem,
        name="info",
    )(days)
    whole = jnp.concatenate([obs, valid.astype(bf16)[None]], axis=0)
    whole = whole.reshape(bands + 1, dates, group, parts, count, width)
    whole = whole.transpose(4, 0, 1, 3, 2, 5)
    whole = whole.reshape(count, size, LANES)
    whole = jnp.concatenate(
        [whole, jnp.broadcast_to(info[None], (count, INFO_ROWS, LANES))], axis=1
    )
    return [lax.dynamic_index_in_dim(whole, me ^ k, 0, keepdims=False) for k in range(count)]


def solve(gram, cross, bands):
    lower = {}
    scaled = {}
    inverse = []
    for col in range(TERMS):
        pivot = gram[col, col] + RIDGE
        for inner in range(col):
            pivot = pivot - lower[col, inner] * scaled[col, inner]
        inverse.append(1.0 / pivot)
        for row in range(col + 1, TERMS):
            entry = gram[col, row]
            for inner in range(col):
                entry = entry - lower[row, inner] * scaled[col, inner]
            scaled[row, col] = entry
            lower[row, col] = entry * inverse[col]
    beta = {}
    for band in range(bands):
        forward = []
        for row in range(TERMS):
            running = cross[row, band]
            for inner in range(row):
                running = running - lower[row, inner] * forward[inner]
            forward.append(running)
        solved = [None] * TERMS
        for row in reversed(range(TERMS)):
            running = forward[row] * inverse[row]
            for inner in range(row + 1, TERMS):
                running = running - lower[inner, row] * solved[inner]
            solved[row] = running
        for row in range(TERMS):
            beta[row, band] = solved[row]
    return beta


def dot(a, b):
    return jnp.dot(a, b, preferred_element_type=f32)


def add_parts(total, size):
    return sum(total[i * size : (i + 1) * size] for i in range(total.shape[0] // size))


def dot_nt(a, b):
    return lax.dot_general(a, b, (((1,), (1,)), ((), ())), preferred_element_type=f32)


def one_hot(shape, first, second):
    row = lax.broadcasted_iota(jnp.int32, shape, 0)
    col = lax.broadcasted_iota(jnp.int32, shape, 1)
    return jnp.where(first(row) == second(col), 1.0, 0.0)


def design_of(infos, dates, parts):
    count = len(infos)
    total = count * dates * parts
    wide = -(-count * dates // LANES) * LANES
    shift = parts.bit_length() - 1
    low_bits = parts - 1
    lane = lax.broadcasted_iota(jnp.int32, (TERMS, LANES), 1)
    sums = [jnp.zeros((TERMS, wide), f32) for _ in range(3)]
    for n, info in enumerate(infos):
        info = info.astype(f32)
        top = info[0:TERMS]
        high = jnp.where(lane < 64, top, 0.0)
        low = jnp.where(lane < 64, pltpu.roll(top, 64, 1), 0.0)
        for c, part in enumerate((high, info[TERMS:], low)):
            if wide > LANES:
                part = jnp.concatenate([part, jnp.zeros((TERMS, wide - LANES), f32)], axis=1)
            if n:
                part = pltpu.roll(part, n * dates, 1)
            sums[c] = sums[c] + part
    x = sums[0] + sums[1] + sums[2]
    stacked = jnp.concatenate(sums + [jnp.zeros((TERMS, wide), f32)], axis=0).astype(bf16)
    spread = one_hot((total, wide), lambda t: t >> shift, lambda d: d).astype(bf16)
    size = TERMS * parts
    repeat = one_hot((3 * size, 4 * TERMS), lambda r: r >> shift, lambda c: c).astype(bf16)
    rows = dot(repeat, stacked)
    same = one_hot((3 * size, total), lambda r: r & low_bits, lambda t: t & low_bits)
    left = (dot_nt(rows.astype(bf16), spread) * same).astype(bf16)
    high, mid, low = rows[0:size], rows[size : 2 * size], rows[2 * size :]
    six = jnp.concatenate([high, mid, low, high, mid, high], axis=0).astype(bf16)
    same = one_hot((total, 6 * size), lambda t: t & low_bits, lambda r: r & low_bits)
    x_wide = (dot_nt(spread, six) * same).astype(bf16)
    products = jnp.concatenate(
        [x[i : i + 1] * x[i:] for i in range(TERMS)] + [jnp.zeros((4, wide), f32)], axis=0
    )
    padded = products.shape[0]
    used = len(pairs) * parts
    product_parts = jnp.concatenate(
        [part.astype(f32) for part in split3_kernel(products)], axis=0
    ).astype(bf16)
    gram_left = []
    same = one_hot((used, total), lambda r: r & low_bits, lambda t: t & low_bits)
    for c in range(3):
        repeat = one_hot((used, 3 * padded), lambda r: (r >> shift) + c * padded, lambda n: n)
        rows = dot(repeat.astype(bf16), product_parts)
        gram_left.append((dot_nt(rows.astype(bf16), spread) * same).astype(bf16))
    return left, gram_left, x_wide


def absorb(blocks, bands, dates, parts, outs, product_ref):
    left_ref, gram_left_ref, x_ref, y_ref, mask_ref = outs
    rows = dates * parts
    left, gram_left, x_wide = design_of(
        [block[(bands + 1) * rows :, :] for block in blocks], dates, parts
    )
    left_ref[...] = left
    x_ref[...] = x_wide
    used = len(pairs) * parts
    for c in range(3):
        gram_left_ref[c * used : (c + 1) * used, :] = gram_left[c]
    for n, block in enumerate(blocks):
        here = slice(n * rows, (n + 1) * rows)
        mask = block[bands * rows : (bands + 1) * rows, :]
        mask_ref[here, :] = mask
        for b in range(bands):
            y = block[b * rows : (b + 1) * rows, :]
            y_ref[here, b * LANES : (b + 1) * LANES] = y
            product_ref[here, b * LANES : (b + 1) * LANES] = y * mask
    cross_sum = add_parts(dot(left_ref[...], product_ref[...]), TERMS * parts)
    gram_sum = add_parts(dot(gram_left_ref[...], mask_ref[...]), used)
    return cross_sum, gram_sum


def single_blocks(refs):
    blocks = []
    for ref in refs:
        blocks += [ref] if len(ref.shape) == 2 else [ref.at[n] for n in range(ref.shape[0])]
    return blocks


def absorb_kernel(shape, *refs):
    bands, dates, parts = shape
    outs, sums, product_ref = refs[-8:-3], refs[-3:-1], refs[-1]
    blocks = single_blocks(refs[:-8])
    cross_sum, gram_sum = absorb(blocks, bands, dates, parts, outs, product_ref)
    sums[0][...] = cross_sum
    sums[1][...] = gram_sum


def fit_and_spread(parts, bands, gram_sum, cross_sum, groups):
    gram = {ij: gram_sum[n * parts : (n + 1) * parts] for n, ij in enumerate(pairs)}
    cross = {
        (k, b): cross_sum[k * parts : (k + 1) * parts, b * LANES : (b + 1) * LANES]
        for k in range(TERMS)
        for b in range(bands)
    }
    beta = solve(gram, cross, bands)
    flat = jnp.concatenate(
        [jnp.concatenate([beta[k, b] for k in range(TERMS)], axis=0) for b in range(bands)], axis=1
    )
    high, mid, low = split3_kernel(flat)
    right = jnp.concatenate([high, high, high, mid, mid, low], axis=0)
    step = 96
    spread = jnp.zeros((8, LANES), f32)
    for y_ref, x_ref, power_ref, weight_of in groups:
        for start in range(0, y_ref.shape[0], step):
            here = slice(start, start + step)
            misfit = y_ref[here, :].astype(f32) - dot(x_ref[here, :], right)
            power = jnp.zeros((step, LANES), f32)
            for b in range(bands):
                part = misfit[:, b * LANES : (b + 1) * LANES]
                power = power + part * part
            power = power / bands
            if power_ref is not None:
                power_ref[here, :] = power
            weighted = weight_of(here) * power
            spread = spread + jnp.sum(weighted.reshape(step // 8, 8, LANES), axis=0)
    spread = add_parts(spread, parts)
    return beta, spread / (1.0 + gram[0, 0])


def first_kernel(shape, arrays, *refs):
    bands, dates, parts = shape
    blocks = single_blocks(refs[:arrays])
    early_x, early_y, early_mask, early_cross, early_gram = refs[arrays : arrays + 5]
    outs = refs[arrays + 5 : arrays + 10]
    early_power, late_power, variance_ref, product_ref = refs[arrays + 10 :]
    cross_sum, gram_sum = absorb(blocks, bands, dates, parts, outs, product_ref)
    _, _, x_ref, y_ref, mask_ref = outs
    groups = [
        (early_y, early_x, early_power, lambda here: early_mask[here, :].astype(f32)),
        (y_ref, x_ref, late_power, lambda here: mask_ref[here, :].astype(f32)),
    ]
    _, variance = fit_and_spread(
        parts, bands, gram_sum + early_gram[...], cross_sum + early_cross[...], groups
    )
    for place in range(variance_ref.shape[0]):
        variance_ref[place] = variance


def smoothed(field_ref, parts, width, rows, spaces, count):
    group = LANES // width
    space = lax.axis_index("space")
    me = lax.axis_index("date")

    def rows_of(space_now, date_now):
        block = field_ref[space_now * count + date_now]
        return [block if h == 0 else pltpu.roll(block, LANES - h * width, 1) for h in range(group)]

    lane = lax.broadcasted_iota(jnp.int32, (rows, LANES), 1)
    sums = []
    for ds in (-1, 0, 1):
        space_now = jnp.clip(space + ds, 0, spaces - 1)
        row_ok = jnp.where((space + ds >= 0) & (space + ds < spaces), 1.0, 0.0)
        across = jnp.zeros((rows, LANES), f32)
        for dd in (-1, 0, 1):
            date_now = jnp.clip(me + dd, 0, count - 1)
            ok = jnp.where((me + dd >= 0) & (me + dd < count), row_ok, 0.0)
            block = jnp.concatenate(rows_of(space_now, date_now), axis=0)
            block = jnp.where(lane < width, block, 0.0) * ok
            for offset in range(-2, 3):
                shift = dd * width - offset
                if abs(shift) >= width and dd * offset <= 0:
                    continue
                moved = block if shift == 0 else pltpu.roll(block, shift % LANES, 1)
                source = lane + offset - dd * width
                across = across + jnp.where((source >= 0) & (source < width), moved, 0.0)
        sums.append(across)
    tall = jnp.concatenate([sums[0][rows - 2 :], sums[1], sums[2][:2]], axis=0)
    total = tall[0:rows]
    for offset in range(1, 5):
        total = total + tall[offset : offset + rows]
    row_index = lax.broadcasted_iota(jnp.int32, (rows, LANES), 0) + space * rows
    col_index = lane + me * width

    def window(index, whole):
        return (jnp.minimum(index + 2, whole - 1) - jnp.maximum(index - 2, 0) + 1).astype(f32)

    smooth = total / (window(row_index, spaces * rows) * window(col_index, count * width))
    return smooth


def to_lanes(tall, parts, width):
    group = LANES // width
    lane = lax.broadcasted_iota(jnp.int32, (parts, LANES), 1)
    out = tall[0:parts]
    for h in range(1, group):
        moved = pltpu.roll(tall[h * parts : (h + 1) * parts], h * width, 1)
        out = jnp.where(lane >= h * width, moved, out)
    return out


def to_rows(block, width):
    group = LANES // width
    tall = [block if h == 0 else pltpu.roll(block, LANES - h * width, 1) for h in range(group)]
    return jnp.concatenate(tall, axis=0)[:, 0:width]


def second_kernel(shape, *refs):
    bands, parts, width, rows, spaces, count = shape
    field_ref = refs[0]
    groups = [refs[1:7], refs[7:13]]
    coefficient_ref, variance_ref = refs[13:15]
    weight_ref, w_parts, wy_parts = refs[15], refs[16:18], refs[18:20]
    smooth = smoothed(field_ref, parts, width, rows, spaces, count)
    smooth = to_lanes(smooth, parts, width)
    scale = 1.0 / (TUKEY * TUKEY * (smooth + EPS))
    scale = jnp.concatenate([scale] * (8 // parts), axis=0)
    early = groups[0][3].shape[0]
    step = 96
    for base, (_, _, _, y_ref, mask_ref, power_ref) in zip((0, early), groups):
        for start in range(0, y_ref.shape[0], step):
            here = slice(start, start + step)
            there = slice(base + start, base + start + step)
            power = power_ref[here, :].reshape(step // 8, 8, LANES)
            left_over = 1.0 - jnp.minimum(power * scale[None], 1.0)
            mask = mask_ref[here, :].astype(f32)
            weight = mask * (left_over * left_over).reshape(step, LANES)
            weight_ref[there, :] = weight
            for ref, part in zip(w_parts, split2_kernel(weight)):
                ref[there, :] = part
            for b in range(bands):
                y = y_ref[here, b * LANES : (b + 1) * LANES].astype(f32)
                for ref, part in zip(wy_parts, split2_kernel(weight * y)):
                    ref[there, b * LANES : (b + 1) * LANES] = part

    def moments(place, b_refs, size):
        total = 0.0
        for base, group in zip((0, early), groups):
            a_ref = group[place]
            there = slice(base, base + group[3].shape[0])
            total = total + add_parts(dot(a_ref[...], b_refs[0][there, :]), size)
            total = total + add_parts(dot(a_ref[0 : 2 * size, :], b_refs[1][there, :]), size)
        return total

    cross_sum = moments(0, wy_parts, TERMS * parts)
    gram_sum = moments(1, w_parts, len(pairs) * parts)
    beta, variance = fit_and_spread(
        parts,
        bands,
        gram_sum,
        cross_sum,
        [
            (groups[0][3], groups[0][2], None, lambda here: weight_ref[here, :]),
            (
                groups[1][3],
                groups[1][2],
                None,
                lambda here: weight_ref[here.start + early : here.stop + early, :],
            ),
        ],
    )
    for place in range(variance_ref.shape[0]):
        variance_ref[place] = variance
    for b in range(bands):
        for k in range(TERMS):
            coefficient_ref[b, k] = to_rows(beta[k, b], width)


def last_kernel(shape, field_ref, noise_ref):
    bands, parts, width, rows, spaces, count = shape
    smooth = smoothed(field_ref, parts, width, rows, spaces, count)
    noise_ref[...] = jnp.sqrt(smooth[:, 0:width] + EPS)


def on_device(obs, valid, days):
    bands, dates, rows, cols = obs.shape
    count = lax.axis_size("date")
    spaces = lax.axis_size("space")
    me = lax.axis_index("date")
    width = cols // count
    group = LANES // width
    parts = rows // group
    half = count // 2
    quarter = half // 2
    early_count, late_count = half + quarter, quarter
    early_rows = early_count * dates * parts
    late_rows = late_count * dates * parts
    shape = (bands, parts, width, rows, spaces, count)
    vmem = pl.BlockSpec(memory_space=pltpu.VMEM)
    params = pltpu.CompilerParams(vmem_limit_bytes=VMEM_BYTES)

    blocks = packed_blocks(obs, valid, days, count, me, width)
    received = [blocks[0]] + [None] * (count - 1)

    def swap(k, after=None):
        block = blocks[k]
        if after is not None:
            block, received[after] = lax.optimization_barrier((block, received[after]))
        received[k] = lax.ppermute(block, "date", [(i, i ^ k) for i in range(count)])

    for k in range(half, count, 2):
        swap(k)
    for k in range(1, half):
        swap(k)
    for k in range(half, count, 2):
        swap(k + 1, after=k ^ 2)

    early_blocks = [*received[:half], *received[half::2]]
    late_blocks = received[half + 1 :: 2]

    def group_shapes(total):
        return [
            jax.ShapeDtypeStruct((3 * TERMS * parts, total), bf16),
            jax.ShapeDtypeStruct((3 * len(pairs) * parts, total), bf16),
            jax.ShapeDtypeStruct((total, 6 * TERMS * parts), bf16),
            jax.ShapeDtypeStruct((total, bands * LANES), bf16),
            jax.ShapeDtypeStruct((total, LANES), bf16),
        ]

    def power(total):
        return jax.ShapeDtypeStruct((total, LANES), f32)

    sums = [
        jax.ShapeDtypeStruct((TERMS * parts, bands * LANES), f32),
        jax.ShapeDtypeStruct((len(pairs) * parts, LANES), f32),
    ]
    send = jax.ShapeDtypeStruct((spaces * count, parts, LANES), f32)
    *early, early_cross, early_gram = pl.pallas_call(
        functools.partial(absorb_kernel, (bands, dates, parts)),
        out_shape=group_shapes(early_rows) + sums,
        in_specs=[vmem] * len(early_blocks),
        out_specs=[vmem] * 7,
        scratch_shapes=[pltpu.VMEM((early_rows, bands * LANES), bf16)],
        compiler_params=params,
        name="absorb",
    )(*early_blocks)
    *late, early_power, late_power, variance = pl.pallas_call(
        functools.partial(first_kernel, (bands, dates, parts), len(late_blocks)),
        out_shape=group_shapes(late_rows) + [power(early_rows), power(late_rows), send],
        in_specs=[vmem] * (len(late_blocks) + 5),
        out_specs=[vmem] * 8,
        scratch_shapes=[pltpu.VMEM((late_rows, bands * LANES), bf16)],
        compiler_params=params,
        name="first",
    )(*late_blocks, early[2], early[3], early[4], early_cross, early_gram)

    field = lax.all_to_all(variance, ("space", "date"), 0, 0, tiled=True)
    total = early_rows + late_rows
    coefficients, variance = pl.pallas_call(
        functools.partial(second_kernel, shape),
        out_shape=[jax.ShapeDtypeStruct((bands, TERMS, rows, width), f32), send],
        in_specs=[vmem] * 13,
        out_specs=[vmem] * 2,
        scratch_shapes=[pltpu.VMEM((total, LANES), f32)]
        + [pltpu.VMEM((total, LANES), bf16)] * 2
        + [pltpu.VMEM((total, bands * LANES), bf16)] * 2,
        compiler_params=params,
        name="second",
    )(field, *early, early_power, *late, late_power)
    field = lax.all_to_all(variance, ("space", "date"), 0, 0, tiled=True)
    noise = pl.pallas_call(
        functools.partial(last_kernel, shape),
        out_shape=jax.ShapeDtypeStruct((rows, width), f32),
        in_specs=[vmem],
        out_specs=vmem,
        compiler_params=params,
        name="last",
    )(field)
    return coefficients, noise


def solution(mesh):
    in_specs = (P(None, "date", "space", None), P("date", "space", None), P("date"))
    out_specs = (P(None, None, "space", "date"), P("space", "date"))
    return jax.shard_map(
        on_device, mesh=mesh, in_specs=in_specs, out_specs=out_specs, check_vma=False
    )
```

```python
import functools
import math

import jax
import jax.numpy as jnp
from jax import lax
from jax.experimental import pallas as pl
from jax.experimental.pallas import tpu as pltpu
from jax.sharding import PartitionSpec as P

TERMS = 8
LANES = 128
TUKEY = 4.685
RIDGE = 1.0
EPS = 1e-06
VMEM_BYTES = 16 * 1024 * 1024
INFO_ROWS = 16
PACK_VMEM_BYTES = 60 * 1024 * 1024
pairs = [(i, j) for i in range(TERMS) for j in range(i, TERMS)]
f32 = jnp.float32
bf16 = jnp.bfloat16


def split2_kernel(x):
    high = x.astype(bf16)
    return high, (x - high.astype(f32)).astype(bf16)


def split3_kernel(x):
    high = x.astype(bf16)
    rest = x - high.astype(f32)
    mid = rest.astype(bf16)
    low = (rest - mid.astype(f32)).astype(bf16)
    return high, mid, low


def design_info(day_ref, dates):
    row = lax.broadcasted_iota(jnp.int32, (TERMS, LANES), 0)
    lane = lax.broadcasted_iota(jnp.int32, (TERMS, LANES), 1)
    day = jnp.zeros((TERMS, LANES), jnp.int32)
    for n in range(dates):
        day = jnp.where(lane == n, day_ref[n], day)
    day = day.astype(f32)
    angle = (row >> 1).astype(f32) * (day * (2.0 * math.pi / 365.25))
    wave = jnp.where((row & 1) == 0, jnp.cos(angle), jnp.sin(angle))
    x = jnp.where(row == 0, 1.0, jnp.where(row == 1, (day - 1825.0) / 1825.0, wave))
    x = jnp.where(lane < dates, x, 0.0)
    high, mid, low = [part.astype(f32) for part in split3_kernel(x)]
    return jnp.concatenate([high + pltpu.roll(low, 64, 1), mid], axis=0).astype(bf16)


def info_kernel(dates, day_ref, out_ref):
    out_ref[...] = design_info(day_ref, dates)


def pack_kernel(steps, far, day_ref, obs_ref, valid_ref, *refs):
    outs = refs[: 2 * len(steps)]
    day_here, obs_here, valid_here, sems, day_sem = refs[-5:]
    me = lax.axis_index("date")
    odd = lax.rem(me, 2) == 1
    bands, dates = obs_ref.shape[:2]
    rows = dates * 4
    day_copy = pltpu.make_async_copy(day_ref, day_here, day_sem)
    day_copy.start()
    arrivals = []
    for place, step in enumerate(steps):
        tile = lax.div(me, 2) ^ step
        lanes = pl.ds(pl.multiple_of(tile * LANES, LANES), LANES)
        arrivals.append(
            (
                pltpu.make_async_copy(
                    obs_ref.at[:, :, :, lanes], obs_here.at[place], sems.at[2 * place]
                ),
                pltpu.make_async_copy(
                    valid_ref.at[:, :, lanes], valid_here.at[place], sems.at[2 * place + 1]
                ),
            )
        )
        for copy in arrivals[place]:
            copy.start()
    day_copy.wait()
    info = design_info(day_here, dates)
    pairs_of_dates = dates // 2
    row = lax.broadcasted_iota(jnp.int32, (pairs_of_dates, 8, LANES), 1)
    lane = lax.broadcasted_iota(jnp.int32, (pairs_of_dates, 8, LANES), 2)
    top = row < 4
    left = lane < 64
    for place, step in enumerate(steps):
        for copy in arrivals[place]:
            copy.wait()
        for band in range(bands + 1):
            block = (obs_here[place, band] if band < bands else valid_here[place]).astype(f32)
            block = block.reshape(pairs_of_dates, 2, 8, LANES)
            first, second = block[:, 0], block[:, 1]

            def turned(x):
                down = pltpu.roll(x, 4, 1)
                return down, pltpu.roll(x, 64, 2), pltpu.roll(down, 64, 2)

            down_1, side_1, both_1 = turned(first)
            down_2, side_2, both_2 = turned(second)
            even_block = jnp.where(
                top, jnp.where(left, first, both_1), jnp.where(left, down_2, side_2)
            )
            odd_block = jnp.where(
                top, jnp.where(left, side_1, down_1), jnp.where(left, both_2, second)
            )
            same = jnp.where(odd, odd_block, even_block)
            other = jnp.where(odd, even_block, odd_block)
            here = slice(band * rows, (band + 1) * rows)
            outs[2 * place][here, :] = same.reshape(rows, LANES).astype(bf16)
            outs[2 * place + 1][here, :] = other.reshape(rows, LANES).astype(bf16)
        outs[2 * place][(bands + 1) * rows :, :] = info
        if not far:
            outs[2 * place + 1][(bands + 1) * rows :, :] = info


def packed_blocks(obs, valid, days, count, me, width):
    bands, dates, rows, cols = obs.shape
    group = LANES // width
    parts = rows // group
    vmem = pl.BlockSpec(memory_space=pltpu.VMEM)
    smem = pl.BlockSpec(memory_space=pltpu.SMEM)
    size = (bands + 1) * dates * parts
    half = count // 2
    if width == 64 and rows == 8:
        hbm = pl.BlockSpec(memory_space=pltpu.HBM)
        blocks = [None] * count
        long_shape = jax.ShapeDtypeStruct((size + INFO_ROWS, LANES), bf16)
        short_shape = jax.ShapeDtypeStruct((size, LANES), bf16)
        for steps in (range(half // 2, half), range(half // 2)):
            tiles = len(steps)
            far = steps[0] > 0
            shapes = [long_shape, short_shape if far else long_shape] * tiles
            given = pl.pallas_call(
                functools.partial(pack_kernel, tuple(steps), far),
                out_shape=shapes,
                in_specs=[hbm] * 3,
                out_specs=[vmem] * len(shapes),
                scratch_shapes=[
                    pltpu.SMEM((dates,), jnp.int32),
                    pltpu.VMEM((tiles, bands, dates, rows, LANES), bf16),
                    pltpu.VMEM((tiles, dates, rows, LANES), jnp.int32),
                    pltpu.SemaphoreType.DMA((2 * tiles,)),
                    pltpu.SemaphoreType.DMA,
                ],
                compiler_params=pltpu.CompilerParams(vmem_limit_bytes=PACK_VMEM_BYTES),
                name="pack",
            )(days, obs, valid)
            blocks[2 * steps[0] : 2 * steps[-1] + 2] = given
        return blocks
    info = pl.pallas_call(
        functools.partial(info_kernel, dates),
        out_shape=jax.ShapeDtypeStruct((INFO_ROWS, LANES), bf16),
        in_specs=[smem],
        out_specs=vmem,
        name="info",
    )(days)
    whole = jnp.concatenate([obs, valid.astype(bf16)[None]], axis=0)
    whole = whole.reshape(bands + 1, dates, group, parts, count, width)
    whole = whole.transpose(4, 0, 1, 3, 2, 5)
    whole = whole.reshape(count, size, LANES)
    whole = jnp.concatenate(
        [whole, jnp.broadcast_to(info[None], (count, INFO_ROWS, LANES))], axis=1
    )
    blocks = [lax.dynamic_index_in_dim(whole, me ^ k, 0, keepdims=False) for k in range(count)]
    blocks[half + 1 :: 2] = [block[:size] for block in blocks[half + 1 :: 2]]
    return blocks


def solve(gram, cross, bands):
    lower = {}
    scaled = {}
    inverse = []
    for col in range(TERMS):
        pivot = gram[col, col] + RIDGE
        for inner in range(col):
            pivot = pivot - lower[col, inner] * scaled[col, inner]
        inverse.append(1.0 / pivot)
        for row in range(col + 1, TERMS):
            entry = gram[col, row]
            for inner in range(col):
                entry = entry - lower[row, inner] * scaled[col, inner]
            scaled[row, col] = entry
            lower[row, col] = entry * inverse[col]
    beta = {}
    for band in range(bands):
        forward = []
        for row in range(TERMS):
            running = cross[row, band]
            for inner in range(row):
                running = running - lower[row, inner] * forward[inner]
            forward.append(running)
        solved = [None] * TERMS
        for row in reversed(range(TERMS)):
            running = forward[row] * inverse[row]
            for inner in range(row + 1, TERMS):
                running = running - lower[inner, row] * solved[inner]
            solved[row] = running
        for row in range(TERMS):
            beta[row, band] = solved[row]
    return beta


def dot(a, b):
    return jnp.dot(a, b, preferred_element_type=f32)


def add_parts(total, size):
    return sum(total[i * size : (i + 1) * size] for i in range(total.shape[0] // size))


def dot_nt(a, b):
    return lax.dot_general(a, b, (((1,), (1,)), ((), ())), preferred_element_type=f32)


def one_hot(shape, first, second):
    row = lax.broadcasted_iota(jnp.int32, shape, 0)
    col = lax.broadcasted_iota(jnp.int32, shape, 1)
    return jnp.where(first(row) == second(col), 1.0, 0.0)


def design_of(infos, dates, parts):
    count = len(infos)
    total = count * dates * parts
    wide = -(-count * dates // LANES) * LANES
    shift = parts.bit_length() - 1
    low_bits = parts - 1
    lane = lax.broadcasted_iota(jnp.int32, (TERMS, LANES), 1)
    sums = [jnp.zeros((TERMS, wide), f32) for _ in range(3)]
    for n, info in enumerate(infos):
        info = info.astype(f32)
        top = info[0:TERMS]
        high = jnp.where(lane < 64, top, 0.0)
        low = jnp.where(lane < 64, pltpu.roll(top, 64, 1), 0.0)
        for c, part in enumerate((high, info[TERMS:], low)):
            if wide > LANES:
                part = jnp.concatenate([part, jnp.zeros((TERMS, wide - LANES), f32)], axis=1)
            if n:
                part = pltpu.roll(part, n * dates, 1)
            sums[c] = sums[c] + part
    x = sums[0] + sums[1] + sums[2]
    stacked = jnp.concatenate(sums + [jnp.zeros((TERMS, wide), f32)], axis=0).astype(bf16)
    spread = one_hot((total, wide), lambda t: t >> shift, lambda d: d).astype(bf16)
    size = TERMS * parts
    repeat = one_hot((3 * size, 4 * TERMS), lambda r: r >> shift, lambda c: c).astype(bf16)
    rows = dot(repeat, stacked)
    same = one_hot((3 * size, total), lambda r: r & low_bits, lambda t: t & low_bits)
    left = (dot_nt(rows.astype(bf16), spread) * same).astype(bf16)
    high, mid, low = rows[0:size], rows[size : 2 * size], rows[2 * size :]
    six = jnp.concatenate([high, mid, low, high, mid, high], axis=0).astype(bf16)
    same = one_hot((total, 6 * size), lambda t: t & low_bits, lambda r: r & low_bits)
    x_wide = (dot_nt(spread, six) * same).astype(bf16)
    products = jnp.concatenate(
        [x[i : i + 1] * x[i:] for i in range(TERMS)] + [jnp.zeros((4, wide), f32)], axis=0
    )
    padded = products.shape[0]
    used = len(pairs) * parts
    product_parts = jnp.concatenate(
        [part.astype(f32) for part in split3_kernel(products)], axis=0
    ).astype(bf16)
    gram_left = []
    same = one_hot((used, total), lambda r: r & low_bits, lambda t: t & low_bits)
    for c in range(3):
        repeat = one_hot((used, 3 * padded), lambda r: (r >> shift) + c * padded, lambda n: n)
        rows = dot(repeat.astype(bf16), product_parts)
        gram_left.append((dot_nt(rows.astype(bf16), spread) * same).astype(bf16))
    return left, gram_left, x_wide


def keep_design(infos, dates, parts, outs):
    left, gram_left, x_wide = design_of(infos, dates, parts)
    used = len(pairs) * parts
    outs[0][...] = left
    for c in range(3):
        outs[1][c * used : (c + 1) * used, :] = gram_left[c]
    outs[2][...] = x_wide


def absorb(blocks, bands, dates, parts, left_ref, gram_left_ref, y_ref, mask_ref, product_ref):
    rows = dates * parts
    for n, block in enumerate(blocks):
        here = slice(n * rows, (n + 1) * rows)
        mask = block[bands * rows : (bands + 1) * rows, :]
        mask_ref[here, :] = mask
        for b in range(bands):
            y = block[b * rows : (b + 1) * rows, :]
            y_ref[here, b * LANES : (b + 1) * LANES] = y
            product_ref[here, b * LANES : (b + 1) * LANES] = y * mask
    cross_sum = add_parts(dot(left_ref[...], product_ref[...]), TERMS * parts)
    gram_sum = add_parts(dot(gram_left_ref[...], mask_ref[...]), len(pairs) * parts)
    return cross_sum, gram_sum


def absorb_kernel(shape, early_count, late_count, *refs):
    bands, dates, parts = shape
    blocks, info_ref = refs[:early_count], refs[early_count]
    infos = [info_ref[n * INFO_ROWS : (n + 1) * INFO_ROWS, :] for n in range(late_count)]
    early, late, sums = refs[-11:-6], refs[-6:-3], refs[-3:-1]
    start = (bands + 1) * dates * parts
    keep_design([block[start:, :] for block in blocks], dates, parts, early[:3])
    keep_design(infos, dates, parts, late)
    sums[0][...], sums[1][...] = absorb(
        blocks, bands, dates, parts, early[0], early[1], early[3], early[4], refs[-1]
    )


def fit_and_spread(parts, bands, gram_sum, cross_sum, groups):
    gram = {ij: gram_sum[n * parts : (n + 1) * parts] for n, ij in enumerate(pairs)}
    cross = {
        (k, b): cross_sum[k * parts : (k + 1) * parts, b * LANES : (b + 1) * LANES]
        for k in range(TERMS)
        for b in range(bands)
    }
    beta = solve(gram, cross, bands)
    flat = jnp.concatenate(
        [jnp.concatenate([beta[k, b] for k in range(TERMS)], axis=0) for b in range(bands)], axis=1
    )
    high, mid, low = split3_kernel(flat)
    right = jnp.concatenate([high, high, high, mid, mid, low], axis=0)
    step = 96
    spread = jnp.zeros((8, LANES), f32)
    for y_ref, x_ref, power_ref, weight_of in groups:
        for start in range(0, y_ref.shape[0], step):
            here = slice(start, start + step)
            misfit = y_ref[here, :].astype(f32) - dot(x_ref[here, :], right)
            power = jnp.zeros((step, LANES), f32)
            for b in range(bands):
                part = misfit[:, b * LANES : (b + 1) * LANES]
                power = power + part * part
            power = power / bands
            if power_ref is not None:
                power_ref[here, :] = power
            weighted = weight_of(here) * power
            spread = spread + jnp.sum(weighted.reshape(step // 8, 8, LANES), axis=0)
    spread = add_parts(spread, parts)
    return beta, spread / (1.0 + gram[0, 0])


def first_kernel(shape, late_count, *refs):
    bands, dates, parts = shape
    blocks = refs[:late_count]
    left_ref, gram_left_ref, x_ref = refs[late_count : late_count + 3]
    early_x, early_y, early_mask, early_cross, early_gram = refs[late_count + 3 : late_count + 8]
    y_ref, mask_ref, early_power, late_power, variance_ref, product_ref = refs[late_count + 8 :]
    cross_sum, gram_sum = absorb(
        blocks, bands, dates, parts, left_ref, gram_left_ref, y_ref, mask_ref, product_ref
    )
    groups = [
        (early_y, early_x, early_power, lambda here: early_mask[here, :].astype(f32)),
        (y_ref, x_ref, late_power, lambda here: mask_ref[here, :].astype(f32)),
    ]
    _, variance = fit_and_spread(
        parts, bands, gram_sum + early_gram[...], cross_sum + early_cross[...], groups
    )
    for place in range(variance_ref.shape[0]):
        variance_ref[place] = variance


def smoothed(field_ref, parts, width, rows, spaces, count):
    group = LANES // width
    space = lax.axis_index("space")
    me = lax.axis_index("date")

    def rows_of(space_now, date_now):
        block = field_ref[space_now * count + date_now]
        return [block if h == 0 else pltpu.roll(block, LANES - h * width, 1) for h in range(group)]

    lane = lax.broadcasted_iota(jnp.int32, (rows, LANES), 1)
    sums = []
    for ds in (-1, 0, 1):
        space_now = jnp.clip(space + ds, 0, spaces - 1)
        row_ok = jnp.where((space + ds >= 0) & (space + ds < spaces), 1.0, 0.0)
        across = jnp.zeros((rows, LANES), f32)
        for dd in (-1, 0, 1):
            date_now = jnp.clip(me + dd, 0, count - 1)
            ok = jnp.where((me + dd >= 0) & (me + dd < count), row_ok, 0.0)
            block = jnp.concatenate(rows_of(space_now, date_now), axis=0)
            block = jnp.where(lane < width, block, 0.0) * ok
            for offset in range(-2, 3):
                shift = dd * width - offset
                if abs(shift) >= width and dd * offset <= 0:
                    continue
                moved = block if shift == 0 else pltpu.roll(block, shift % LANES, 1)
                source = lane + offset - dd * width
                across = across + jnp.where((source >= 0) & (source < width), moved, 0.0)
        sums.append(across)
    tall = jnp.concatenate([sums[0][rows - 2 :], sums[1], sums[2][:2]], axis=0)
    total = tall[0:rows]
    for offset in range(1, 5):
        total = total + tall[offset : offset + rows]
    row_index = lax.broadcasted_iota(jnp.int32, (rows, LANES), 0) + space * rows
    col_index = lane + me * width

    def window(index, whole):
        return (jnp.minimum(index + 2, whole - 1) - jnp.maximum(index - 2, 0) + 1).astype(f32)

    smooth = total / (window(row_index, spaces * rows) * window(col_index, count * width))
    return smooth


def to_lanes(tall, parts, width):
    group = LANES // width
    lane = lax.broadcasted_iota(jnp.int32, (parts, LANES), 1)
    out = tall[0:parts]
    for h in range(1, group):
        moved = pltpu.roll(tall[h * parts : (h + 1) * parts], h * width, 1)
        out = jnp.where(lane >= h * width, moved, out)
    return out


def to_rows(block, width):
    group = LANES // width
    tall = [block if h == 0 else pltpu.roll(block, LANES - h * width, 1) for h in range(group)]
    return jnp.concatenate(tall, axis=0)[:, 0:width]


def second_kernel(shape, *refs):
    bands, parts, width, rows, spaces, count = shape
    field_ref = refs[0]
    groups = [refs[1:7], refs[7:13]]
    coefficient_ref, variance_ref = refs[13:15]
    weight_ref, w_parts, wy_parts = refs[15], refs[16:18], refs[18:20]
    smooth = smoothed(field_ref, parts, width, rows, spaces, count)
    smooth = to_lanes(smooth, parts, width)
    scale = 1.0 / (TUKEY * TUKEY * (smooth + EPS))
    scale = jnp.concatenate([scale] * (8 // parts), axis=0)
    early = groups[0][3].shape[0]
    step = 96
    for base, (_, _, _, y_ref, mask_ref, power_ref) in zip((0, early), groups):
        for start in range(0, y_ref.shape[0], step):
            here = slice(start, start + step)
            there = slice(base + start, base + start + step)
            power = power_ref[here, :].reshape(step // 8, 8, LANES)
            left_over = 1.0 - jnp.minimum(power * scale[None], 1.0)
            mask = mask_ref[here, :].astype(f32)
            weight = mask * (left_over * left_over).reshape(step, LANES)
            weight_ref[there, :] = weight
            for ref, part in zip(w_parts, split2_kernel(weight)):
                ref[there, :] = part
            for b in range(bands):
                y = y_ref[here, b * LANES : (b + 1) * LANES].astype(f32)
                for ref, part in zip(wy_parts, split2_kernel(weight * y)):
                    ref[there, b * LANES : (b + 1) * LANES] = part

    def moments(place, b_refs, size):
        total = 0.0
        for base, group in zip((0, early), groups):
            a_ref = group[place]
            there = slice(base, base + group[3].shape[0])
            total = total + add_parts(dot(a_ref[...], b_refs[0][there, :]), size)
            total = total + add_parts(dot(a_ref[0 : 2 * size, :], b_refs[1][there, :]), size)
        return total

    cross_sum = moments(0, wy_parts, TERMS * parts)
    gram_sum = moments(1, w_parts, len(pairs) * parts)
    beta, variance = fit_and_spread(
        parts,
        bands,
        gram_sum,
        cross_sum,
        [
            (groups[0][3], groups[0][2], None, lambda here: weight_ref[here, :]),
            (
                groups[1][3],
                groups[1][2],
                None,
                lambda here: weight_ref[here.start + early : here.stop + early, :],
            ),
        ],
    )
    for place in range(variance_ref.shape[0]):
        variance_ref[place] = variance
    for b in range(bands):
        for k in range(TERMS):
            coefficient_ref[b, k] = to_rows(beta[k, b], width)


def last_kernel(shape, field_ref, noise_ref):
    bands, parts, width, rows, spaces, count = shape
    smooth = smoothed(field_ref, parts, width, rows, spaces, count)
    noise_ref[...] = jnp.sqrt(smooth[:, 0:width] + EPS)


def on_device(obs, valid, days):
    bands, dates, rows, cols = obs.shape
    count = lax.axis_size("date")
    spaces = lax.axis_size("space")
    me = lax.axis_index("date")
    width = cols // count
    group = LANES // width
    parts = rows // group
    half = count // 2
    quarter = half // 2
    early_count, late_count = half + quarter, quarter
    early_rows = early_count * dates * parts
    late_rows = late_count * dates * parts
    shape = (bands, parts, width, rows, spaces, count)
    vmem = pl.BlockSpec(memory_space=pltpu.VMEM)
    params = pltpu.CompilerParams(vmem_limit_bytes=VMEM_BYTES)

    blocks = packed_blocks(obs, valid, days, count, me, width)
    received = [blocks[0]] + [None] * (count - 1)

    def swap(k, after=None):
        block = blocks[k]
        if after is not None:
            block, received[after] = lax.optimization_barrier((block, received[after]))
        received[k] = lax.ppermute(block, "date", [(i, i ^ k) for i in range(count)])

    for k in range(half, count, 2):
        swap(k)
    for k in range(1, half):
        swap(k)
    for k in range(half, count, 2):
        swap(k + 1, after=k ^ 2)

    infos = jnp.concatenate([block[-INFO_ROWS:] for block in received[half::2]], axis=0)
    infos = lax.ppermute(infos, "date", [(i, i ^ 1) for i in range(count)])
    early_blocks = [*received[:half], *received[half::2]]
    late_blocks = received[half + 1 :: 2]

    def design_shapes(total):
        return [
            jax.ShapeDtypeStruct((3 * TERMS * parts, total), bf16),
            jax.ShapeDtypeStruct((3 * len(pairs) * parts, total), bf16),
            jax.ShapeDtypeStruct((total, 6 * TERMS * parts), bf16),
        ]

    def data_shapes(total):
        return [
            jax.ShapeDtypeStruct((total, bands * LANES), bf16),
            jax.ShapeDtypeStruct((total, LANES), bf16),
        ]

    def power(total):
        return jax.ShapeDtypeStruct((total, LANES), f32)

    sums = [
        jax.ShapeDtypeStruct((TERMS * parts, bands * LANES), f32),
        jax.ShapeDtypeStruct((len(pairs) * parts, LANES), f32),
    ]
    send = jax.ShapeDtypeStruct((spaces * count, parts, LANES), f32)
    given = pl.pallas_call(
        functools.partial(absorb_kernel, (bands, dates, parts), early_count, late_count),
        out_shape=design_shapes(early_rows)
        + data_shapes(early_rows)
        + design_shapes(late_rows)
        + sums,
        in_specs=[vmem] * (early_count + 1),
        out_specs=[vmem] * 10,
        scratch_shapes=[pltpu.VMEM((early_rows, bands * LANES), bf16)],
        compiler_params=params,
        name="absorb",
    )(*early_blocks, infos)
    early, late, early_sums = given[:5], given[5:8], given[8:]
    *late_data, early_power, late_power, variance = pl.pallas_call(
        functools.partial(first_kernel, (bands, dates, parts), late_count),
        out_shape=data_shapes(late_rows) + [power(early_rows), power(late_rows), send],
        in_specs=[vmem] * (late_count + 8),
        out_specs=[vmem] * 5,
        scratch_shapes=[pltpu.VMEM((late_rows, bands * LANES), bf16)],
        compiler_params=params,
        name="first",
    )(*late_blocks, *late, *early[2:], *early_sums)
    late = [*late, *late_data]

    field = lax.all_to_all(variance, ("space", "date"), 0, 0, tiled=True)
    total = early_rows + late_rows
    coefficients, variance = pl.pallas_call(
        functools.partial(second_kernel, shape),
        out_shape=[jax.ShapeDtypeStruct((bands, TERMS, rows, width), f32), send],
        in_specs=[vmem] * 13,
        out_specs=[vmem] * 2,
        scratch_shapes=[pltpu.VMEM((total, LANES), f32)]
        + [pltpu.VMEM((total, LANES), bf16)] * 2
        + [pltpu.VMEM((total, bands * LANES), bf16)] * 2,
        compiler_params=params,
        name="second",
    )(field, *early, early_power, *late, late_power)
    field = lax.all_to_all(variance, ("space", "date"), 0, 0, tiled=True)
    noise = pl.pallas_call(
        functools.partial(last_kernel, shape),
        out_shape=jax.ShapeDtypeStruct((rows, width), f32),
        in_specs=[vmem],
        out_specs=vmem,
        compiler_params=params,
        name="last",
    )(field)
    return coefficients, noise


def solution(mesh):
    in_specs = (P(None, "date", "space", None), P("date", "space", None), P("date"))
    out_specs = (P(None, None, "space", "date"), P("space", "date"))
    return jax.shard_map(
        on_device, mesh=mesh, in_specs=in_specs, out_specs=out_specs, check_vma=False
    )
```

```python
import functools
import math

import jax
import jax.numpy as jnp
from jax import lax
from jax.experimental import pallas as pl
from jax.experimental.pallas import tpu as pltpu
from jax.sharding import PartitionSpec as P

TERMS = 8
LANES = 128
TUKEY = 4.685
RIDGE = 1.0
EPS = 1e-06
VMEM_BYTES = 16 * 1024 * 1024
INFO_ROWS = 16
PACK_VMEM_BYTES = 60 * 1024 * 1024
pairs = [(i, j) for i in range(TERMS) for j in range(i, TERMS)]
f32 = jnp.float32
bf16 = jnp.bfloat16


def split2_kernel(x):
    high = x.astype(bf16)
    return high, (x - high.astype(f32)).astype(bf16)


def split3_kernel(x):
    high = x.astype(bf16)
    rest = x - high.astype(f32)
    mid = rest.astype(bf16)
    low = (rest - mid.astype(f32)).astype(bf16)
    return high, mid, low


def design_info(day_ref, dates):
    row = lax.broadcasted_iota(jnp.int32, (TERMS, LANES), 0)
    lane = lax.broadcasted_iota(jnp.int32, (TERMS, LANES), 1)
    day = jnp.zeros((TERMS, LANES), jnp.int32)
    for n in range(dates):
        day = jnp.where(lane == n, day_ref[n], day)
    day = day.astype(f32)
    angle = (row >> 1).astype(f32) * (day * (2.0 * math.pi / 365.25))
    wave = jnp.where((row & 1) == 0, jnp.cos(angle), jnp.sin(angle))
    x = jnp.where(row == 0, 1.0, jnp.where(row == 1, (day - 1825.0) / 1825.0, wave))
    x = jnp.where(lane < dates, x, 0.0)
    high, mid, low = [part.astype(f32) for part in split3_kernel(x)]
    return jnp.concatenate([high + pltpu.roll(low, 64, 1), mid], axis=0).astype(bf16)


def info_kernel(dates, day_ref, out_ref):
    out_ref[...] = design_info(day_ref, dates)


def pack_kernel(steps, far, day_ref, obs_ref, valid_ref, *refs):
    outs = refs[: 2 * len(steps)]
    day_here, obs_here, valid_here, sems, day_sem = refs[-5:]
    me = lax.axis_index("date")
    odd = lax.rem(me, 2) == 1
    bands, dates = obs_ref.shape[:2]
    rows = dates * 4
    day_copy = pltpu.make_async_copy(day_ref, day_here, day_sem)
    day_copy.start()
    arrivals = []
    for place, step in enumerate(steps):
        tile = lax.div(me, 2) ^ step
        lanes = pl.ds(pl.multiple_of(tile * LANES, LANES), LANES)
        arrivals.append(
            (
                pltpu.make_async_copy(
                    obs_ref.at[:, :, :, lanes], obs_here.at[place], sems.at[2 * place]
                ),
                pltpu.make_async_copy(
                    valid_ref.at[:, :, lanes], valid_here.at[place], sems.at[2 * place + 1]
                ),
            )
        )
        for copy in arrivals[place]:
            copy.start()
    day_copy.wait()
    info = design_info(day_here, dates)
    pairs_of_dates = dates // 2
    row = lax.broadcasted_iota(jnp.int32, (pairs_of_dates, 8, LANES), 1)
    lane = lax.broadcasted_iota(jnp.int32, (pairs_of_dates, 8, LANES), 2)
    top = row < 4
    left = lane < 64
    for place, step in enumerate(steps):
        for copy in arrivals[place]:
            copy.wait()
        for band in range(bands + 1):
            block = (obs_here[place, band] if band < bands else valid_here[place]).astype(f32)
            block = block.reshape(pairs_of_dates, 2, 8, LANES)
            first, second = block[:, 0], block[:, 1]

            def turned(x):
                down = pltpu.roll(x, 4, 1)
                return down, pltpu.roll(x, 64, 2), pltpu.roll(down, 64, 2)

            down_1, side_1, both_1 = turned(first)
            down_2, side_2, both_2 = turned(second)
            even_block = jnp.where(
                top, jnp.where(left, first, both_1), jnp.where(left, down_2, side_2)
            )
            odd_block = jnp.where(
                top, jnp.where(left, side_1, down_1), jnp.where(left, both_2, second)
            )
            same = jnp.where(odd, odd_block, even_block)
            other = jnp.where(odd, even_block, odd_block)
            here = slice(band * rows, (band + 1) * rows)
            outs[2 * place][here, :] = same.reshape(rows, LANES).astype(bf16)
            outs[2 * place + 1][here, :] = other.reshape(rows, LANES).astype(bf16)
        outs[2 * place][(bands + 1) * rows :, :] = info
        if not far:
            outs[2 * place + 1][(bands + 1) * rows :, :] = info


def packed_blocks(obs, valid, days, count, me, width):
    bands, dates, rows, cols = obs.shape
    group = LANES // width
    parts = rows // group
    vmem = pl.BlockSpec(memory_space=pltpu.VMEM)
    smem = pl.BlockSpec(memory_space=pltpu.SMEM)
    size = (bands + 1) * dates * parts
    half = count // 2
    if width == 64 and rows == 8:
        hbm = pl.BlockSpec(memory_space=pltpu.HBM)
        blocks = [None] * count
        long_shape = jax.ShapeDtypeStruct((size + INFO_ROWS, LANES), bf16)
        short_shape = jax.ShapeDtypeStruct((size, LANES), bf16)
        for steps in (range(half // 2, half), range(half // 2)):
            tiles = len(steps)
            far = steps[0] > 0
            shapes = [long_shape, short_shape if far else long_shape] * tiles
            given = pl.pallas_call(
                functools.partial(pack_kernel, tuple(steps), far),
                out_shape=shapes,
                in_specs=[hbm] * 3,
                out_specs=[vmem] * len(shapes),
                scratch_shapes=[
                    pltpu.SMEM((dates,), jnp.int32),
                    pltpu.VMEM((tiles, bands, dates, rows, LANES), bf16),
                    pltpu.VMEM((tiles, dates, rows, LANES), jnp.int32),
                    pltpu.SemaphoreType.DMA((2 * tiles,)),
                    pltpu.SemaphoreType.DMA,
                ],
                compiler_params=pltpu.CompilerParams(vmem_limit_bytes=PACK_VMEM_BYTES),
                name="pack",
            )(days, obs, valid)
            blocks[2 * steps[0] : 2 * steps[-1] + 2] = given
        return blocks
    info = pl.pallas_call(
        functools.partial(info_kernel, dates),
        out_shape=jax.ShapeDtypeStruct((INFO_ROWS, LANES), bf16),
        in_specs=[smem],
        out_specs=vmem,
        name="info",
    )(days)
    whole = jnp.concatenate([obs, valid.astype(bf16)[None]], axis=0)
    whole = whole.reshape(bands + 1, dates, group, parts, count, width)
    whole = whole.transpose(4, 0, 1, 3, 2, 5)
    whole = whole.reshape(count, size, LANES)
    whole = jnp.concatenate(
        [whole, jnp.broadcast_to(info[None], (count, INFO_ROWS, LANES))], axis=1
    )
    blocks = [lax.dynamic_index_in_dim(whole, me ^ k, 0, keepdims=False) for k in range(count)]
    blocks[half + 1 :: 2] = [block[:size] for block in blocks[half + 1 :: 2]]
    return blocks


def solve(gram, cross, bands):
    lower = {}
    scaled = {}
    inverse = []
    for col in range(TERMS):
        pivot = gram[col, col] + RIDGE
        for inner in range(col):
            pivot = pivot - lower[col, inner] * scaled[col, inner]
        inverse.append(1.0 / pivot)
        for row in range(col + 1, TERMS):
            entry = gram[col, row]
            for inner in range(col):
                entry = entry - lower[row, inner] * scaled[col, inner]
            scaled[row, col] = entry
            lower[row, col] = entry * inverse[col]
    beta = {}
    for band in range(bands):
        forward = []
        for row in range(TERMS):
            running = cross[row, band]
            for inner in range(row):
                running = running - lower[row, inner] * forward[inner]
            forward.append(running)
        solved = [None] * TERMS
        for row in reversed(range(TERMS)):
            running = forward[row] * inverse[row]
            for inner in range(row + 1, TERMS):
                running = running - lower[inner, row] * solved[inner]
            solved[row] = running
        for row in range(TERMS):
            beta[row, band] = solved[row]
    return beta


def dot(a, b):
    return jnp.dot(a, b, preferred_element_type=f32)


def add_parts(total, size):
    return sum(total[i * size : (i + 1) * size] for i in range(total.shape[0] // size))


def dot_nt(a, b):
    return lax.dot_general(a, b, (((1,), (1,)), ((), ())), preferred_element_type=f32)


def one_hot(shape, first, second):
    row = lax.broadcasted_iota(jnp.int32, shape, 0)
    col = lax.broadcasted_iota(jnp.int32, shape, 1)
    return jnp.where(first(row) == second(col), 1.0, 0.0)


def design_of(infos, dates, parts):
    count = len(infos)
    total = count * dates * parts
    wide = -(-count * dates // LANES) * LANES
    shift = parts.bit_length() - 1
    low_bits = parts - 1
    lane = lax.broadcasted_iota(jnp.int32, (TERMS, LANES), 1)
    sums = [jnp.zeros((TERMS, wide), f32) for _ in range(3)]
    for n, info in enumerate(infos):
        info = info.astype(f32)
        top = info[0:TERMS]
        high = jnp.where(lane < 64, top, 0.0)
        low = jnp.where(lane < 64, pltpu.roll(top, 64, 1), 0.0)
        for c, part in enumerate((high, info[TERMS:], low)):
            if wide > LANES:
                part = jnp.concatenate([part, jnp.zeros((TERMS, wide - LANES), f32)], axis=1)
            if n:
                part = pltpu.roll(part, n * dates, 1)
            sums[c] = sums[c] + part
    x = sums[0] + sums[1] + sums[2]
    stacked = jnp.concatenate(sums + [jnp.zeros((TERMS, wide), f32)], axis=0).astype(bf16)
    spread = one_hot((total, wide), lambda t: t >> shift, lambda d: d).astype(bf16)
    size = TERMS * parts
    repeat = one_hot((3 * size, 4 * TERMS), lambda r: r >> shift, lambda c: c).astype(bf16)
    rows = dot(repeat, stacked)
    same = one_hot((3 * size, total), lambda r: r & low_bits, lambda t: t & low_bits)
    left = (dot_nt(rows.astype(bf16), spread) * same).astype(bf16)
    high, mid, low = rows[0:size], rows[size : 2 * size], rows[2 * size :]
    six = jnp.concatenate([high, mid, low, high, mid, high], axis=0).astype(bf16)
    same = one_hot((total, 6 * size), lambda t: t & low_bits, lambda r: r & low_bits)
    x_wide = (dot_nt(spread, six) * same).astype(bf16)
    products = jnp.concatenate(
        [x[i : i + 1] * x[i:] for i in range(TERMS)] + [jnp.zeros((4, wide), f32)], axis=0
    )
    padded = products.shape[0]
    used = len(pairs) * parts
    product_parts = jnp.concatenate(
        [part.astype(f32) for part in split3_kernel(products)], axis=0
    ).astype(bf16)
    gram_left = []
    same = one_hot((used, total), lambda r: r & low_bits, lambda t: t & low_bits)
    for c in range(3):
        repeat = one_hot((used, 3 * padded), lambda r: (r >> shift) + c * padded, lambda n: n)
        rows = dot(repeat.astype(bf16), product_parts)
        gram_left.append((dot_nt(rows.astype(bf16), spread) * same).astype(bf16))
    return left, gram_left, x_wide


def keep_design(infos, dates, parts, outs):
    left, gram_left, x_wide = design_of(infos, dates, parts)
    used = len(pairs) * parts
    outs[0][...] = left
    for c in range(3):
        outs[1][c * used : (c + 1) * used, :] = gram_left[c]
    outs[2][...] = x_wide


def absorb(blocks, bands, dates, parts, left_ref, gram_left_ref, y_ref, mask_ref):
    rows = dates * parts
    masks = []
    products = []
    for n, block in enumerate(blocks):
        here = slice(n * rows, (n + 1) * rows)
        mask = block[bands * rows : (bands + 1) * rows, :]
        mask_ref[here, :] = mask
        masks.append(mask)
        product = []
        for b in range(bands):
            y = block[b * rows : (b + 1) * rows, :]
            y_ref[here, b * LANES : (b + 1) * LANES] = y
            product.append(y * mask)
        products.append(jnp.concatenate(product, axis=1))
    product = jnp.concatenate(products, axis=0)
    cross_sum = add_parts(dot(left_ref[...], product), TERMS * parts)
    gram_sum = add_parts(dot(gram_left_ref[...], jnp.concatenate(masks, axis=0)), len(pairs) * parts)
    return cross_sum, gram_sum


def absorb_kernel(shape, early_count, late_count, *refs):
    bands, dates, parts = shape
    blocks, info_ref = refs[:early_count], refs[early_count]
    infos = [info_ref[n * INFO_ROWS : (n + 1) * INFO_ROWS, :] for n in range(late_count)]
    early, late, sums = refs[-10:-5], refs[-5:-2], refs[-2:]
    start = (bands + 1) * dates * parts
    keep_design([block[start:, :] for block in blocks], dates, parts, early[:3])
    keep_design(infos, dates, parts, late)
    sums[0][...], sums[1][...] = absorb(
        blocks, bands, dates, parts, early[0], early[1], early[3], early[4]
    )


def fit_and_spread(parts, bands, gram_sum, cross_sum, groups):
    gram = {ij: gram_sum[n * parts : (n + 1) * parts] for n, ij in enumerate(pairs)}
    cross = {
        (k, b): cross_sum[k * parts : (k + 1) * parts, b * LANES : (b + 1) * LANES]
        for k in range(TERMS)
        for b in range(bands)
    }
    beta = solve(gram, cross, bands)
    flat = jnp.concatenate(
        [jnp.concatenate([beta[k, b] for k in range(TERMS)], axis=0) for b in range(bands)], axis=1
    )
    high, mid, low = split3_kernel(flat)
    right = jnp.concatenate([high, high, high, mid, mid, low], axis=0)
    spread = jnp.zeros((8, LANES), f32)
    for y_ref, x_ref, power_ref, weight_of in groups:
        size = y_ref.shape[0]
        misfit = y_ref[...].astype(f32) - dot(x_ref[...], right)
        power = jnp.zeros((size, LANES), f32)
        for b in range(bands):
            part = misfit[:, b * LANES : (b + 1) * LANES]
            power = power + part * part
        power = power / bands
        if power_ref is not None:
            power_ref[...] = power
        weighted = weight_of() * power
        spread = spread + jnp.sum(weighted.reshape(size // 8, 8, LANES), axis=0)
    spread = add_parts(spread, parts)
    return beta, spread / (1.0 + gram[0, 0])


def first_kernel(shape, late_count, *refs):
    bands, dates, parts = shape
    blocks = refs[:late_count]
    left_ref, gram_left_ref, x_ref = refs[late_count : late_count + 3]
    early_x, early_y, early_mask, early_cross, early_gram = refs[late_count + 3 : late_count + 8]
    y_ref, mask_ref, early_power, late_power, variance_ref = refs[late_count + 8 :]
    cross_sum, gram_sum = absorb(
        blocks, bands, dates, parts, left_ref, gram_left_ref, y_ref, mask_ref
    )
    groups = [
        (early_y, early_x, early_power, lambda: early_mask[...].astype(f32)),
        (y_ref, x_ref, late_power, lambda: mask_ref[...].astype(f32)),
    ]
    _, variance = fit_and_spread(
        parts, bands, gram_sum + early_gram[...], cross_sum + early_cross[...], groups
    )
    for place in range(variance_ref.shape[0]):
        variance_ref[place] = variance


def smoothed(field_ref, parts, width, rows, spaces, count):
    group = LANES // width
    space = lax.axis_index("space")
    me = lax.axis_index("date")

    def rows_of(space_now, date_now):
        block = field_ref[space_now * count + date_now]
        return [block if h == 0 else pltpu.roll(block, LANES - h * width, 1) for h in range(group)]

    lane = lax.broadcasted_iota(jnp.int32, (rows, LANES), 1)
    sums = []
    for ds in (-1, 0, 1):
        space_now = jnp.clip(space + ds, 0, spaces - 1)
        row_ok = jnp.where((space + ds >= 0) & (space + ds < spaces), 1.0, 0.0)
        across = jnp.zeros((rows, LANES), f32)
        for dd in (-1, 0, 1):
            date_now = jnp.clip(me + dd, 0, count - 1)
            ok = jnp.where((me + dd >= 0) & (me + dd < count), row_ok, 0.0)
            block = jnp.concatenate(rows_of(space_now, date_now), axis=0)
            block = jnp.where(lane < width, block, 0.0) * ok
            for offset in range(-2, 3):
                shift = dd * width - offset
                if abs(shift) >= width and dd * offset <= 0:
                    continue
                moved = block if shift == 0 else pltpu.roll(block, shift % LANES, 1)
                source = lane + offset - dd * width
                across = across + jnp.where((source >= 0) & (source < width), moved, 0.0)
        sums.append(across)
    tall = jnp.concatenate([sums[0][rows - 2 :], sums[1], sums[2][:2]], axis=0)
    total = tall[0:rows]
    for offset in range(1, 5):
        total = total + tall[offset : offset + rows]
    row_index = lax.broadcasted_iota(jnp.int32, (rows, LANES), 0) + space * rows
    col_index = lane + me * width

    def window(index, whole):
        return (jnp.minimum(index + 2, whole - 1) - jnp.maximum(index - 2, 0) + 1).astype(f32)

    smooth = total / (window(row_index, spaces * rows) * window(col_index, count * width))
    return smooth


def to_lanes(tall, parts, width):
    group = LANES // width
    lane = lax.broadcasted_iota(jnp.int32, (parts, LANES), 1)
    out = tall[0:parts]
    for h in range(1, group):
        moved = pltpu.roll(tall[h * parts : (h + 1) * parts], h * width, 1)
        out = jnp.where(lane >= h * width, moved, out)
    return out


def to_rows(block, width):
    group = LANES // width
    tall = [block if h == 0 else pltpu.roll(block, LANES - h * width, 1) for h in range(group)]
    return jnp.concatenate(tall, axis=0)[:, 0:width]


def second_kernel(shape, *refs):
    bands, parts, width, rows, spaces, count = shape
    field_ref = refs[0]
    groups = [refs[1:7], refs[7:13]]
    coefficient_ref, variance_ref = refs[13:15]
    weight_ref = refs[15]
    smooth = smoothed(field_ref, parts, width, rows, spaces, count)
    smooth = to_lanes(smooth, parts, width)
    scale = 1.0 / (TUKEY * TUKEY * (smooth + EPS))
    scale = jnp.concatenate([scale] * (8 // parts), axis=0)
    early = groups[0][3].shape[0]
    cross_sum = gram_sum = 0.0
    for base, (left_ref, gram_left_ref, _, y_ref, mask_ref, power_ref) in zip((0, early), groups):
        size = y_ref.shape[0]
        power = power_ref[...].reshape(size // 8, 8, LANES)
        left_over = 1.0 - jnp.minimum(power * scale[None], 1.0)
        mask = mask_ref[...].astype(f32)
        weight = mask * (left_over * left_over).reshape(size, LANES)
        weight_ref[base : base + size, :] = weight
        wy_parts = [[], []]
        for b in range(bands):
            y = y_ref[:, b * LANES : (b + 1) * LANES].astype(f32)
            for n, part in enumerate(split2_kernel(weight * y)):
                wy_parts[n].append(part)
        wy_parts = [jnp.concatenate(part, axis=1) for part in wy_parts]

        def moments(a_ref, b_parts, used):
            total = add_parts(dot(a_ref[...], b_parts[0]), used)
            return total + add_parts(dot(a_ref[0 : 2 * used, :], b_parts[1]), used)

        cross_sum = cross_sum + moments(left_ref, wy_parts, TERMS * parts)
        gram_sum = gram_sum + moments(gram_left_ref, split2_kernel(weight), len(pairs) * parts)

    beta, variance = fit_and_spread(
        parts,
        bands,
        gram_sum,
        cross_sum,
        [
            (groups[0][3], groups[0][2], None, lambda: weight_ref[0:early, :]),
            (
                groups[1][3],
                groups[1][2],
                None,
                lambda: weight_ref[early:, :],
            ),
        ],
    )
    for place in range(variance_ref.shape[0]):
        variance_ref[place] = variance
    for b in range(bands):
        for k in range(TERMS):
            coefficient_ref[b, k] = to_rows(beta[k, b], width)


def last_kernel(shape, field_ref, noise_ref):
    bands, parts, width, rows, spaces, count = shape
    smooth = smoothed(field_ref, parts, width, rows, spaces, count)
    noise_ref[...] = jnp.sqrt(smooth[:, 0:width] + EPS)


def on_device(obs, valid, days):
    bands, dates, rows, cols = obs.shape
    count = lax.axis_size("date")
    spaces = lax.axis_size("space")
    me = lax.axis_index("date")
    width = cols // count
    group = LANES // width
    parts = rows // group
    half = count // 2
    quarter = half // 2
    early_count, late_count = half + quarter, quarter
    early_rows = early_count * dates * parts
    late_rows = late_count * dates * parts
    shape = (bands, parts, width, rows, spaces, count)
    vmem = pl.BlockSpec(memory_space=pltpu.VMEM)
    params = pltpu.CompilerParams(vmem_limit_bytes=VMEM_BYTES)

    blocks = packed_blocks(obs, valid, days, count, me, width)
    received = [blocks[0]] + [None] * (count - 1)

    def swap(k, after=None):
        block = blocks[k]
        if after is not None:
            block, received[after] = lax.optimization_barrier((block, received[after]))
        received[k] = lax.ppermute(block, "date", [(i, i ^ k) for i in range(count)])

    for k in range(half, count, 2):
        swap(k)
    for k in range(1, half):
        swap(k)
    for k in range(half, count, 2):
        swap(k + 1, after=k ^ 2)

    infos = jnp.concatenate([block[-INFO_ROWS:] for block in received[half::2]], axis=0)
    infos = lax.ppermute(infos, "date", [(i, i ^ 1) for i in range(count)])
    early_blocks = [*received[:half], *received[half::2]]
    late_blocks = received[half + 1 :: 2]

    def design_shapes(total):
        return [
            jax.ShapeDtypeStruct((3 * TERMS * parts, total), bf16),
            jax.ShapeDtypeStruct((3 * len(pairs) * parts, total), bf16),
            jax.ShapeDtypeStruct((total, 6 * TERMS * parts), bf16),
        ]

    def data_shapes(total):
        return [
            jax.ShapeDtypeStruct((total, bands * LANES), bf16),
            jax.ShapeDtypeStruct((total, LANES), bf16),
        ]

    def power(total):
        return jax.ShapeDtypeStruct((total, LANES), f32)

    sums = [
        jax.ShapeDtypeStruct((TERMS * parts, bands * LANES), f32),
        jax.ShapeDtypeStruct((len(pairs) * parts, LANES), f32),
    ]
    send = jax.ShapeDtypeStruct((spaces * count, parts, LANES), f32)
    given = pl.pallas_call(
        functools.partial(absorb_kernel, (bands, dates, parts), early_count, late_count),
        out_shape=design_shapes(early_rows)
        + data_shapes(early_rows)
        + design_shapes(late_rows)
        + sums,
        in_specs=[vmem] * (early_count + 1),
        out_specs=[vmem] * 10,
        compiler_params=params,
        name="absorb",
    )(*early_blocks, infos)
    early, late, early_sums = given[:5], given[5:8], given[8:]
    *late_data, early_power, late_power, variance = pl.pallas_call(
        functools.partial(first_kernel, (bands, dates, parts), late_count),
        out_shape=data_shapes(late_rows) + [power(early_rows), power(late_rows), send],
        in_specs=[vmem] * (late_count + 8),
        out_specs=[vmem] * 5,
        compiler_params=params,
        name="first",
    )(*late_blocks, *late, *early[2:], *early_sums)
    late = [*late, *late_data]

    field = lax.all_to_all(variance, ("space", "date"), 0, 0, tiled=True)
    total = early_rows + late_rows
    coefficients, variance = pl.pallas_call(
        functools.partial(second_kernel, shape),
        out_shape=[jax.ShapeDtypeStruct((bands, TERMS, rows, width), f32), send],
        in_specs=[vmem] * 13,
        out_specs=[vmem] * 2,
        scratch_shapes=[pltpu.VMEM((total, LANES), f32)],
        compiler_params=params,
        name="second",
    )(field, *early, early_power, *late, late_power)
    field = lax.all_to_all(variance, ("space", "date"), 0, 0, tiled=True)
    noise = pl.pallas_call(
        functools.partial(last_kernel, shape),
        out_shape=jax.ShapeDtypeStruct((rows, width), f32),
        in_specs=[vmem],
        out_specs=vmem,
        compiler_params=params,
        name="last",
    )(field)
    return coefficients, noise


def solution(mesh):
    in_specs = (P(None, "date", "space", None), P("date", "space", None), P("date"))
    out_specs = (P(None, None, "space", "date"), P("space", "date"))
    return jax.shard_map(
        on_device, mesh=mesh, in_specs=in_specs, out_specs=out_specs, check_vma=False
    )
```

```python
import functools
import math

import jax
import jax.numpy as jnp
from jax import lax
from jax.experimental import pallas as pl
from jax.experimental.pallas import tpu as pltpu
from jax.sharding import PartitionSpec as P

TERMS = 8
LANES = 128
TUKEY = 4.685
RIDGE = 1.0
EPS = 1e-06
VMEM_BYTES = 16 * 1024 * 1024
INFO_ROWS = 16
PACK_VMEM_BYTES = 60 * 1024 * 1024
pairs = [(i, j) for i in range(TERMS) for j in range(i, TERMS)]
f32 = jnp.float32
bf16 = jnp.bfloat16


def split2_kernel(x):
    high = x.astype(bf16)
    return high, (x - high.astype(f32)).astype(bf16)


def split3_kernel(x):
    high = x.astype(bf16)
    rest = x - high.astype(f32)
    mid = rest.astype(bf16)
    low = (rest - mid.astype(f32)).astype(bf16)
    return high, mid, low


def design_info(day_ref, dates):
    row = lax.broadcasted_iota(jnp.int32, (TERMS, LANES), 0)
    lane = lax.broadcasted_iota(jnp.int32, (TERMS, LANES), 1)
    day = jnp.zeros((TERMS, LANES), jnp.int32)
    for n in range(dates):
        day = jnp.where(lane == n, day_ref[n], day)
    day = day.astype(f32)
    angle = (row >> 1).astype(f32) * (day * (2.0 * math.pi / 365.25))
    wave = jnp.where((row & 1) == 0, jnp.cos(angle), jnp.sin(angle))
    x = jnp.where(row == 0, 1.0, jnp.where(row == 1, (day - 1825.0) / 1825.0, wave))
    x = jnp.where(lane < dates, x, 0.0)
    high, mid, low = [part.astype(f32) for part in split3_kernel(x)]
    return jnp.concatenate([high + pltpu.roll(low, 64, 1), mid], axis=0).astype(bf16)


def info_kernel(dates, day_ref, out_ref):
    out_ref[...] = design_info(day_ref, dates)


def pack_kernel(steps, far, day_ref, obs_ref, valid_ref, *refs):
    outs = refs[: 2 * len(steps)]
    day_here, obs_here, valid_here, sems, day_sem = refs[-5:]
    me = lax.axis_index("date")
    odd = lax.rem(me, 2) == 1
    bands, dates = obs_ref.shape[:2]
    rows = dates * 4
    day_copy = pltpu.make_async_copy(day_ref, day_here, day_sem)
    day_copy.start()
    arrivals = []
    for place, step in enumerate(steps):
        tile = lax.div(me, 2) ^ step
        lanes = pl.ds(pl.multiple_of(tile * LANES, LANES), LANES)
        arrivals.append(
            (
                pltpu.make_async_copy(
                    obs_ref.at[:, :, :, lanes], obs_here.at[place], sems.at[2 * place]
                ),
                pltpu.make_async_copy(
                    valid_ref.at[:, :, lanes], valid_here.at[place], sems.at[2 * place + 1]
                ),
            )
        )
        for copy in arrivals[place]:
            copy.start()
    day_copy.wait()
    info = design_info(day_here, dates)
    pairs_of_dates = dates // 2
    row = lax.broadcasted_iota(jnp.int32, (pairs_of_dates, 8, LANES), 1)
    lane = lax.broadcasted_iota(jnp.int32, (pairs_of_dates, 8, LANES), 2)
    top = row < 4
    left = lane < 64
    for place, step in enumerate(steps):
        for copy in arrivals[place]:
            copy.wait()
        for band in range(bands + 1):
            block = (obs_here[place, band] if band < bands else valid_here[place]).astype(f32)
            block = block.reshape(pairs_of_dates, 2, 8, LANES)
            first, second = block[:, 0], block[:, 1]

            def turned(x):
                down = pltpu.roll(x, 4, 1)
                return down, pltpu.roll(x, 64, 2), pltpu.roll(down, 64, 2)

            down_1, side_1, both_1 = turned(first)
            down_2, side_2, both_2 = turned(second)
            even_block = jnp.where(
                top, jnp.where(left, first, both_1), jnp.where(left, down_2, side_2)
            )
            odd_block = jnp.where(
                top, jnp.where(left, side_1, down_1), jnp.where(left, both_2, second)
            )
            same = jnp.where(odd, odd_block, even_block)
            other = jnp.where(odd, even_block, odd_block)
            here = slice(band * rows, (band + 1) * rows)
            outs[2 * place][here, :] = same.reshape(rows, LANES).astype(bf16)
            outs[2 * place + 1][here, :] = other.reshape(rows, LANES).astype(bf16)
        outs[2 * place][(bands + 1) * rows :, :] = info
        if not far:
            outs[2 * place + 1][(bands + 1) * rows :, :] = info


def packed_blocks(obs, valid, days, count, me, width):
    bands, dates, rows, cols = obs.shape
    group = LANES // width
    parts = rows // group
    vmem = pl.BlockSpec(memory_space=pltpu.VMEM)
    smem = pl.BlockSpec(memory_space=pltpu.SMEM)
    size = (bands + 1) * dates * parts
    half = count // 2
    if width == 64 and rows == 8:
        hbm = pl.BlockSpec(memory_space=pltpu.HBM)
        blocks = [None] * count
        long_shape = jax.ShapeDtypeStruct((size + INFO_ROWS, LANES), bf16)
        short_shape = jax.ShapeDtypeStruct((size, LANES), bf16)
        for steps in (range(half // 2, half), range(half // 2)):
            tiles = len(steps)
            far = steps[0] > 0
            shapes = [long_shape, short_shape if far else long_shape] * tiles
            given = pl.pallas_call(
                functools.partial(pack_kernel, tuple(steps), far),
                out_shape=shapes,
                in_specs=[hbm] * 3,
                out_specs=[vmem] * len(shapes),
                scratch_shapes=[
                    pltpu.SMEM((dates,), jnp.int32),
                    pltpu.VMEM((tiles, bands, dates, rows, LANES), bf16),
                    pltpu.VMEM((tiles, dates, rows, LANES), jnp.int32),
                    pltpu.SemaphoreType.DMA((2 * tiles,)),
                    pltpu.SemaphoreType.DMA,
                ],
                compiler_params=pltpu.CompilerParams(vmem_limit_bytes=PACK_VMEM_BYTES),
                name="pack",
            )(days, obs, valid)
            blocks[2 * steps[0] : 2 * steps[-1] + 2] = given
        return blocks
    info = pl.pallas_call(
        functools.partial(info_kernel, dates),
        out_shape=jax.ShapeDtypeStruct((INFO_ROWS, LANES), bf16),
        in_specs=[smem],
        out_specs=vmem,
        name="info",
    )(days)
    whole = jnp.concatenate([obs, valid.astype(bf16)[None]], axis=0)
    whole = whole.reshape(bands + 1, dates, group, parts, count, width)
    whole = whole.transpose(4, 0, 1, 3, 2, 5)
    whole = whole.reshape(count, size, LANES)
    whole = jnp.concatenate(
        [whole, jnp.broadcast_to(info[None], (count, INFO_ROWS, LANES))], axis=1
    )
    blocks = [lax.dynamic_index_in_dim(whole, me ^ k, 0, keepdims=False) for k in range(count)]
    blocks[half + 1 :: 2] = [block[:size] for block in blocks[half + 1 :: 2]]
    return blocks


def solve(gram, cross, bands):
    lower = {}
    scaled = {}
    inverse = []
    for col in range(TERMS):
        pivot = gram[col, col] + RIDGE
        for inner in range(col):
            pivot = pivot - lower[col, inner] * scaled[col, inner]
        inverse.append(1.0 / pivot)
        for row in range(col + 1, TERMS):
            entry = gram[col, row]
            for inner in range(col):
                entry = entry - lower[row, inner] * scaled[col, inner]
            scaled[row, col] = entry
            lower[row, col] = entry * inverse[col]
    beta = {}
    for band in range(bands):
        forward = []
        for row in range(TERMS):
            running = cross[row, band]
            for inner in range(row):
                running = running - lower[row, inner] * forward[inner]
            forward.append(running)
        solved = [None] * TERMS
        for row in reversed(range(TERMS)):
            running = forward[row] * inverse[row]
            for inner in range(row + 1, TERMS):
                running = running - lower[inner, row] * solved[inner]
            solved[row] = running
        for row in range(TERMS):
            beta[row, band] = solved[row]
    return beta


def dot(a, b):
    return jnp.dot(a, b, preferred_element_type=f32)


def add_parts(total, size):
    return sum(total[i * size : (i + 1) * size] for i in range(total.shape[0] // size))


def dot_nt(a, b):
    return lax.dot_general(a, b, (((1,), (1,)), ((), ())), preferred_element_type=f32)


def one_hot(shape, first, second):
    row = lax.broadcasted_iota(jnp.int32, shape, 0)
    col = lax.broadcasted_iota(jnp.int32, shape, 1)
    return jnp.where(first(row) == second(col), 1.0, 0.0)


def design_of(infos, dates, parts):
    count = len(infos)
    total = count * dates * parts
    wide = -(-count * dates // LANES) * LANES
    shift = parts.bit_length() - 1
    low_bits = parts - 1
    lane = lax.broadcasted_iota(jnp.int32, (TERMS, LANES), 1)
    sums = [jnp.zeros((TERMS, wide), f32) for _ in range(3)]
    for n, info in enumerate(infos):
        info = info.astype(f32)
        top = info[0:TERMS]
        high = jnp.where(lane < 64, top, 0.0)
        low = jnp.where(lane < 64, pltpu.roll(top, 64, 1), 0.0)
        for c, part in enumerate((high, info[TERMS:], low)):
            if wide > LANES:
                part = jnp.concatenate([part, jnp.zeros((TERMS, wide - LANES), f32)], axis=1)
            if n:
                part = pltpu.roll(part, n * dates, 1)
            sums[c] = sums[c] + part
    x = sums[0] + sums[1] + sums[2]
    stacked = jnp.concatenate(sums + [jnp.zeros((TERMS, wide), f32)], axis=0).astype(bf16)
    spread = one_hot((total, wide), lambda t: t >> shift, lambda d: d).astype(bf16)
    size = TERMS * parts
    repeat = one_hot((3 * size, 4 * TERMS), lambda r: r >> shift, lambda c: c).astype(bf16)
    rows = dot(repeat, stacked)
    same = one_hot((3 * size, total), lambda r: r & low_bits, lambda t: t & low_bits)
    left = (dot_nt(rows.astype(bf16), spread) * same).astype(bf16)
    high, mid, low = rows[0:size], rows[size : 2 * size], rows[2 * size :]
    six = jnp.concatenate([high, mid, low, high, mid, high], axis=0).astype(bf16)
    same = one_hot((total, 6 * size), lambda t: t & low_bits, lambda r: r & low_bits)
    x_wide = (dot_nt(spread, six) * same).astype(bf16)
    products = jnp.concatenate(
        [x[i : i + 1] * x[i:] for i in range(TERMS)] + [jnp.zeros((4, wide), f32)], axis=0
    )
    padded = products.shape[0]
    used = len(pairs) * parts
    product_parts = jnp.concatenate(
        [part.astype(f32) for part in split3_kernel(products)], axis=0
    ).astype(bf16)
    gram_left = []
    same = one_hot((used, total), lambda r: r & low_bits, lambda t: t & low_bits)
    for c in range(3):
        repeat = one_hot((used, 3 * padded), lambda r: (r >> shift) + c * padded, lambda n: n)
        rows = dot(repeat.astype(bf16), product_parts)
        gram_left.append((dot_nt(rows.astype(bf16), spread) * same).astype(bf16))
    return left, gram_left, x_wide


def keep_design(infos, dates, parts, outs):
    left, gram_left, x_wide = design_of(infos, dates, parts)
    used = len(pairs) * parts
    outs[0][...] = left
    for c in range(3):
        outs[1][c * used : (c + 1) * used, :] = gram_left[c]
    outs[2][...] = x_wide


def absorb(blocks, bands, dates, parts, left_ref, gram_left_ref, y_ref, mask_ref):
    rows = dates * parts
    masks = []
    products = []
    for n, block in enumerate(blocks):
        here = slice(n * rows, (n + 1) * rows)
        mask = block[bands * rows : (bands + 1) * rows, :]
        mask_ref[here, :] = mask
        masks.append(mask)
        product = []
        for b in range(bands):
            y = block[b * rows : (b + 1) * rows, :]
            y_ref[here, b * LANES : (b + 1) * LANES] = y
            product.append(y * mask)
        products.append(jnp.concatenate(product, axis=1))
    product = jnp.concatenate(products, axis=0)
    cross_sum = add_parts(dot(left_ref[...], product), TERMS * parts)
    gram_sum = add_parts(dot(gram_left_ref[...], jnp.concatenate(masks, axis=0)), len(pairs) * parts)
    return cross_sum, gram_sum


def absorb_kernel(shape, early_count, late_count, *refs):
    bands, dates, parts = shape
    blocks, info_ref = refs[:early_count], refs[early_count]
    infos = [info_ref[n * INFO_ROWS : (n + 1) * INFO_ROWS, :] for n in range(late_count)]
    early, late, sums = refs[-10:-5], refs[-5:-2], refs[-2:]
    start = (bands + 1) * dates * parts
    keep_design([block[start:, :] for block in blocks], dates, parts, early[:3])
    keep_design(infos, dates, parts, late)
    sums[0][...], sums[1][...] = absorb(
        blocks, bands, dates, parts, early[0], early[1], early[3], early[4]
    )


def fit_and_spread(parts, bands, gram_sum, cross_sum, groups):
    gram = {ij: gram_sum[n * parts : (n + 1) * parts] for n, ij in enumerate(pairs)}
    cross = {
        (k, b): cross_sum[k * parts : (k + 1) * parts, b * LANES : (b + 1) * LANES]
        for k in range(TERMS)
        for b in range(bands)
    }
    beta = solve(gram, cross, bands)
    flat = jnp.concatenate(
        [jnp.concatenate([beta[k, b] for k in range(TERMS)], axis=0) for b in range(bands)], axis=1
    )
    high, mid, low = split3_kernel(flat)
    right = jnp.concatenate([high, high, high, mid, mid, low], axis=0)
    spread = jnp.zeros((8, LANES), f32)
    for y_ref, x_ref, power_ref, weight_of in groups:
        size = y_ref.shape[0]
        misfit = y_ref[...].astype(f32) - dot(x_ref[...], right)
        power = jnp.zeros((size, LANES), f32)
        for b in range(bands):
            part = misfit[:, b * LANES : (b + 1) * LANES]
            power = power + part * part
        if power_ref is not None:
            power_ref[...] = power
        weighted = weight_of() * power
        spread = spread + jnp.sum(weighted.reshape(size // 8, 8, LANES), axis=0)
    spread = add_parts(spread, parts)
    return beta, spread / (bands * (1.0 + gram[0, 0]))


def first_kernel(shape, late_count, *refs):
    bands, dates, parts = shape
    blocks = refs[:late_count]
    left_ref, gram_left_ref, x_ref = refs[late_count : late_count + 3]
    early_x, early_y, early_mask, early_cross, early_gram = refs[late_count + 3 : late_count + 8]
    y_ref, mask_ref, early_power, late_power, variance_ref = refs[late_count + 8 :]
    cross_sum, gram_sum = absorb(
        blocks, bands, dates, parts, left_ref, gram_left_ref, y_ref, mask_ref
    )
    groups = [
        (early_y, early_x, early_power, lambda: early_mask[...].astype(f32)),
        (y_ref, x_ref, late_power, lambda: mask_ref[...].astype(f32)),
    ]
    _, variance = fit_and_spread(
        parts, bands, gram_sum + early_gram[...], cross_sum + early_cross[...], groups
    )
    for place in range(variance_ref.shape[0]):
        variance_ref[place] = variance


def smoothed(field_ref, parts, width, rows, spaces, count):
    group = LANES // width
    space = lax.axis_index("space")
    me = lax.axis_index("date")

    def rows_of(space_now, date_now):
        block = field_ref[space_now * count + date_now]
        return [block if h == 0 else pltpu.roll(block, LANES - h * width, 1) for h in range(group)]

    lane = lax.broadcasted_iota(jnp.int32, (rows, LANES), 1)
    sums = []
    for ds in (-1, 0, 1):
        space_now = jnp.clip(space + ds, 0, spaces - 1)
        row_ok = jnp.where((space + ds >= 0) & (space + ds < spaces), 1.0, 0.0)
        across = jnp.zeros((rows, LANES), f32)
        for dd in (-1, 0, 1):
            date_now = jnp.clip(me + dd, 0, count - 1)
            ok = jnp.where((me + dd >= 0) & (me + dd < count), row_ok, 0.0)
            block = jnp.concatenate(rows_of(space_now, date_now), axis=0)
            block = jnp.where(lane < width, block, 0.0) * ok
            for offset in range(-2, 3):
                shift = dd * width - offset
                if abs(shift) >= width and dd * offset <= 0:
                    continue
                moved = block if shift == 0 else pltpu.roll(block, shift % LANES, 1)
                source = lane + offset - dd * width
                across = across + jnp.where((source >= 0) & (source < width), moved, 0.0)
        sums.append(across)
    tall = jnp.concatenate([sums[0][rows - 2 :], sums[1], sums[2][:2]], axis=0)
    total = tall[0:rows]
    for offset in range(1, 5):
        total = total + tall[offset : offset + rows]
    row_index = lax.broadcasted_iota(jnp.int32, (rows, LANES), 0) + space * rows
    col_index = lane + me * width

    def window(index, whole):
        return (jnp.minimum(index + 2, whole - 1) - jnp.maximum(index - 2, 0) + 1).astype(f32)

    smooth = total / (window(row_index, spaces * rows) * window(col_index, count * width))
    return smooth


def to_lanes(tall, parts, width):
    group = LANES // width
    lane = lax.broadcasted_iota(jnp.int32, (parts, LANES), 1)
    out = tall[0:parts]
    for h in range(1, group):
        moved = pltpu.roll(tall[h * parts : (h + 1) * parts], h * width, 1)
        out = jnp.where(lane >= h * width, moved, out)
    return out


def to_rows(block, width):
    group = LANES // width
    tall = [block if h == 0 else pltpu.roll(block, LANES - h * width, 1) for h in range(group)]
    return jnp.concatenate(tall, axis=0)[:, 0:width]


def second_kernel(shape, *refs):
    bands, parts, width, rows, spaces, count = shape
    field_ref = refs[0]
    groups = [refs[1:7], refs[7:13]]
    coefficient_ref, variance_ref = refs[13:15]
    weight_ref = refs[15]
    smooth = smoothed(field_ref, parts, width, rows, spaces, count)
    smooth = to_lanes(smooth, parts, width)
    scale = 1.0 / (bands * (TUKEY * TUKEY) * (smooth + EPS))
    scale = jnp.concatenate([scale] * (8 // parts), axis=0)
    early = groups[0][3].shape[0]
    cross_sum = gram_sum = 0.0
    for base, (left_ref, gram_left_ref, _, y_ref, mask_ref, power_ref) in zip((0, early), groups):
        size = y_ref.shape[0]
        power = power_ref[...].reshape(size // 8, 8, LANES)
        left_over = 1.0 - jnp.minimum(power * scale[None], 1.0)
        mask = mask_ref[...].astype(f32)
        weight = mask * (left_over * left_over).reshape(size, LANES)
        weight_ref[base : base + size, :] = weight
        wy_parts = [[], []]
        for b in range(bands):
            y = y_ref[:, b * LANES : (b + 1) * LANES].astype(f32)
            for n, part in enumerate(split2_kernel(weight * y)):
                wy_parts[n].append(part)
        wy_parts = [jnp.concatenate(part, axis=1) for part in wy_parts]

        def moments(a_ref, b_parts, used):
            total = add_parts(dot(a_ref[...], b_parts[0]), used)
            return total + add_parts(dot(a_ref[0 : 2 * used, :], b_parts[1]), used)

        gram_sum = gram_sum + moments(gram_left_ref, split2_kernel(weight), len(pairs) * parts)
        cross_sum = cross_sum + moments(left_ref, wy_parts, TERMS * parts)

    beta, variance = fit_and_spread(
        parts,
        bands,
        gram_sum,
        cross_sum,
        [
            (groups[0][3], groups[0][2], None, lambda: weight_ref[0:early, :]),
            (
                groups[1][3],
                groups[1][2],
                None,
                lambda: weight_ref[early:, :],
            ),
        ],
    )
    for place in range(variance_ref.shape[0]):
        variance_ref[place] = variance
    for b in range(bands):
        for k in range(TERMS):
            coefficient_ref[b, k] = to_rows(beta[k, b], width)


def last_kernel(shape, field_ref, noise_ref):
    bands, parts, width, rows, spaces, count = shape
    smooth = smoothed(field_ref, parts, width, rows, spaces, count)
    noise_ref[...] = jnp.sqrt(smooth[:, 0:width] + EPS)


def on_device(obs, valid, days):
    bands, dates, rows, cols = obs.shape
    count = lax.axis_size("date")
    spaces = lax.axis_size("space")
    me = lax.axis_index("date")
    width = cols // count
    group = LANES // width
    parts = rows // group
    half = count // 2
    quarter = half // 2
    early_count, late_count = half + quarter, quarter
    early_rows = early_count * dates * parts
    late_rows = late_count * dates * parts
    shape = (bands, parts, width, rows, spaces, count)
    vmem = pl.BlockSpec(memory_space=pltpu.VMEM)
    params = pltpu.CompilerParams(vmem_limit_bytes=VMEM_BYTES)

    blocks = packed_blocks(obs, valid, days, count, me, width)
    received = [blocks[0]] + [None] * (count - 1)

    def swap(k, after=None):
        block = blocks[k]
        if after is not None:
            block, received[after] = lax.optimization_barrier((block, received[after]))
        received[k] = lax.ppermute(block, "date", [(i, i ^ k) for i in range(count)])

    for k in range(half, count, 2):
        swap(k)
    for k in range(1, half):
        swap(k)
    for k in range(half, count, 2):
        swap(k + 1, after=k ^ 2)

    infos = jnp.concatenate([block[-INFO_ROWS:] for block in received[half::2]], axis=0)
    infos = lax.ppermute(infos, "date", [(i, i ^ 1) for i in range(count)])
    early_blocks = [*received[:half], *received[half::2]]
    late_blocks = received[half + 1 :: 2]

    def design_shapes(total):
        return [
            jax.ShapeDtypeStruct((3 * TERMS * parts, total), bf16),
            jax.ShapeDtypeStruct((3 * len(pairs) * parts, total), bf16),
            jax.ShapeDtypeStruct((total, 6 * TERMS * parts), bf16),
        ]

    def data_shapes(total):
        return [
            jax.ShapeDtypeStruct((total, bands * LANES), bf16),
            jax.ShapeDtypeStruct((total, LANES), bf16),
        ]

    def power(total):
        return jax.ShapeDtypeStruct((total, LANES), f32)

    sums = [
        jax.ShapeDtypeStruct((TERMS * parts, bands * LANES), f32),
        jax.ShapeDtypeStruct((len(pairs) * parts, LANES), f32),
    ]
    send = jax.ShapeDtypeStruct((spaces * count, parts, LANES), f32)
    given = pl.pallas_call(
        functools.partial(absorb_kernel, (bands, dates, parts), early_count, late_count),
        out_shape=design_shapes(early_rows)
        + data_shapes(early_rows)
        + design_shapes(late_rows)
        + sums,
        in_specs=[vmem] * (early_count + 1),
        out_specs=[vmem] * 10,
        compiler_params=params,
        name="absorb",
    )(*early_blocks, infos)
    early, late, early_sums = given[:5], given[5:8], given[8:]
    *late_data, early_power, late_power, variance = pl.pallas_call(
        functools.partial(first_kernel, (bands, dates, parts), late_count),
        out_shape=data_shapes(late_rows) + [power(early_rows), power(late_rows), send],
        in_specs=[vmem] * (late_count + 8),
        out_specs=[vmem] * 5,
        compiler_params=params,
        name="first",
    )(*late_blocks, *late, *early[2:], *early_sums)
    late = [*late, *late_data]

    field = lax.all_to_all(variance, ("space", "date"), 0, 0, tiled=True)
    total = early_rows + late_rows
    coefficients, variance = pl.pallas_call(
        functools.partial(second_kernel, shape),
        out_shape=[jax.ShapeDtypeStruct((bands, TERMS, rows, width), f32), send],
        in_specs=[vmem] * 13,
        out_specs=[vmem] * 2,
        scratch_shapes=[pltpu.VMEM((total, LANES), f32)],
        compiler_params=params,
        name="second",
    )(field, *early, early_power, *late, late_power)
    field = lax.all_to_all(variance, ("space", "date"), 0, 0, tiled=True)
    noise = pl.pallas_call(
        functools.partial(last_kernel, shape),
        out_shape=jax.ShapeDtypeStruct((rows, width), f32),
        in_specs=[vmem],
        out_specs=vmem,
        compiler_params=params,
        name="last",
    )(field)
    return coefficients, noise


def solution(mesh):
    in_specs = (P(None, "date", "space", None), P("date", "space", None), P("date"))
    out_specs = (P(None, None, "space", "date"), P("space", "date"))
    return jax.shard_map(
        on_device, mesh=mesh, in_specs=in_specs, out_specs=out_specs, check_vma=False
    )
```

```python
import functools
import math

import jax
import jax.numpy as jnp
from jax import lax
from jax.experimental import pallas as pl
from jax.experimental.pallas import tpu as pltpu
from jax.sharding import PartitionSpec as P

TERMS = 8
LANES = 128
TUKEY = 4.685
RIDGE = 1.0
EPS = 1e-06
VMEM_BYTES = 16 * 1024 * 1024
INFO_ROWS = 16
PACK_VMEM_BYTES = 60 * 1024 * 1024
pairs = [(i, j) for i in range(TERMS) for j in range(i, TERMS)]
f32 = jnp.float32
bf16 = jnp.bfloat16


def split2_kernel(x):
    high = x.astype(bf16)
    return high, (x - high.astype(f32)).astype(bf16)


def split3_kernel(x):
    high = x.astype(bf16)
    rest = x - high.astype(f32)
    mid = rest.astype(bf16)
    low = (rest - mid.astype(f32)).astype(bf16)
    return high, mid, low


def design_info(day_ref, dates):
    row = lax.broadcasted_iota(jnp.int32, (TERMS, LANES), 0)
    lane = lax.broadcasted_iota(jnp.int32, (TERMS, LANES), 1)
    day = jnp.zeros((TERMS, LANES), jnp.int32)
    for n in range(dates):
        day = jnp.where(lane == n, day_ref[n], day)
    day = day.astype(f32)
    angle = (row >> 1).astype(f32) * (day * (2.0 * math.pi / 365.25))
    wave = jnp.where((row & 1) == 0, jnp.cos(angle), jnp.sin(angle))
    x = jnp.where(row == 0, 1.0, jnp.where(row == 1, (day - 1825.0) / 1825.0, wave))
    x = jnp.where(lane < dates, x, 0.0)
    high, mid, low = [part.astype(f32) for part in split3_kernel(x)]
    return jnp.concatenate([high + pltpu.roll(low, 64, 1), mid], axis=0).astype(bf16)


def info_kernel(dates, day_ref, out_ref):
    out_ref[...] = design_info(day_ref, dates)


def pack_kernel(steps, far, day_ref, obs_ref, valid_ref, *refs):
    outs = refs[: 2 * len(steps)]
    day_here, obs_here, valid_here, sems, day_sem = refs[-5:]
    me = lax.axis_index("date")
    odd = lax.rem(me, 2) == 1
    bands, dates = obs_ref.shape[:2]
    rows = dates * 4
    day_copy = pltpu.make_async_copy(day_ref, day_here, day_sem)
    day_copy.start()
    arrivals = []
    for place, step in enumerate(steps):
        tile = lax.div(me, 2) ^ step
        lanes = pl.ds(pl.multiple_of(tile * LANES, LANES), LANES)
        arrivals.append(
            (
                pltpu.make_async_copy(
                    obs_ref.at[:, :, :, lanes], obs_here.at[place], sems.at[2 * place]
                ),
                pltpu.make_async_copy(
                    valid_ref.at[:, :, lanes], valid_here.at[place], sems.at[2 * place + 1]
                ),
            )
        )
        for copy in arrivals[place]:
            copy.start()
    day_copy.wait()
    info = design_info(day_here, dates)
    pairs_of_dates = dates // 2
    row = lax.broadcasted_iota(jnp.int32, (pairs_of_dates, 8, LANES), 1)
    lane = lax.broadcasted_iota(jnp.int32, (pairs_of_dates, 8, LANES), 2)
    top = row < 4
    left = lane < 64
    for place, step in enumerate(steps):
        for copy in arrivals[place]:
            copy.wait()
        for band in range(bands + 1):
            block = (obs_here[place, band] if band < bands else valid_here[place]).astype(f32)
            block = block.reshape(pairs_of_dates, 2, 8, LANES)
            first, second = block[:, 0], block[:, 1]

            def turned(x):
                down = pltpu.roll(x, 4, 1)
                return down, pltpu.roll(x, 64, 2), pltpu.roll(down, 64, 2)

            down_1, side_1, both_1 = turned(first)
            down_2, side_2, both_2 = turned(second)
            even_block = jnp.where(
                top, jnp.where(left, first, both_1), jnp.where(left, down_2, side_2)
            )
            odd_block = jnp.where(
                top, jnp.where(left, side_1, down_1), jnp.where(left, both_2, second)
            )
            same = jnp.where(odd, odd_block, even_block)
            other = jnp.where(odd, even_block, odd_block)
            here = slice(band * rows, (band + 1) * rows)
            outs[2 * place][here, :] = same.reshape(rows, LANES).astype(bf16)
            outs[2 * place + 1][here, :] = other.reshape(rows, LANES).astype(bf16)
        outs[2 * place][(bands + 1) * rows :, :] = info
        if not far:
            outs[2 * place + 1][(bands + 1) * rows :, :] = info


def packed_blocks(obs, valid, days, count, me, width):
    bands, dates, rows, cols = obs.shape
    group = LANES // width
    parts = rows // group
    vmem = pl.BlockSpec(memory_space=pltpu.VMEM)
    smem = pl.BlockSpec(memory_space=pltpu.SMEM)
    size = (bands + 1) * dates * parts
    half = count // 2
    if width == 64 and rows == 8:
        hbm = pl.BlockSpec(memory_space=pltpu.HBM)
        blocks = [None] * count
        long_shape = jax.ShapeDtypeStruct((size + INFO_ROWS, LANES), bf16)
        short_shape = jax.ShapeDtypeStruct((size, LANES), bf16)
        for steps in (range(half // 2, half), range(half // 2)):
            tiles = len(steps)
            far = steps[0] > 0
            shapes = [long_shape, short_shape if far else long_shape] * tiles
            given = pl.pallas_call(
                functools.partial(pack_kernel, tuple(steps), far),
                out_shape=shapes,
                in_specs=[hbm] * 3,
                out_specs=[vmem] * len(shapes),
                scratch_shapes=[
                    pltpu.SMEM((dates,), jnp.int32),
                    pltpu.VMEM((tiles, bands, dates, rows, LANES), bf16),
                    pltpu.VMEM((tiles, dates, rows, LANES), jnp.int32),
                    pltpu.SemaphoreType.DMA((2 * tiles,)),
                    pltpu.SemaphoreType.DMA,
                ],
                compiler_params=pltpu.CompilerParams(vmem_limit_bytes=PACK_VMEM_BYTES),
                name="pack",
            )(days, obs, valid)
            blocks[2 * steps[0] : 2 * steps[-1] + 2] = given
        return blocks
    info = pl.pallas_call(
        functools.partial(info_kernel, dates),
        out_shape=jax.ShapeDtypeStruct((INFO_ROWS, LANES), bf16),
        in_specs=[smem],
        out_specs=vmem,
        name="info",
    )(days)
    whole = jnp.concatenate([obs, valid.astype(bf16)[None]], axis=0)
    whole = whole.reshape(bands + 1, dates, group, parts, count, width)
    whole = whole.transpose(4, 0, 1, 3, 2, 5)
    whole = whole.reshape(count, size, LANES)
    whole = jnp.concatenate(
        [whole, jnp.broadcast_to(info[None], (count, INFO_ROWS, LANES))], axis=1
    )
    blocks = [lax.dynamic_index_in_dim(whole, me ^ k, 0, keepdims=False) for k in range(count)]
    blocks[half + 1 :: 2] = [block[:size] for block in blocks[half + 1 :: 2]]
    return blocks


def solve(gram, cross, bands):
    lower = {}
    scaled = {}
    inverse = []
    for col in range(TERMS):
        pivot = gram[col, col] + RIDGE
        for inner in range(col):
            pivot = pivot - lower[col, inner] * scaled[col, inner]
        inverse.append(1.0 / pivot)
        for row in range(col + 1, TERMS):
            entry = gram[col, row]
            for inner in range(col):
                entry = entry - lower[row, inner] * scaled[col, inner]
            scaled[row, col] = entry
            lower[row, col] = entry * inverse[col]
    beta = {}
    for band in range(bands):
        forward = []
        for row in range(TERMS):
            running = cross[row, band]
            for inner in range(row):
                running = running - lower[row, inner] * forward[inner]
            forward.append(running)
        solved = [None] * TERMS
        for row in reversed(range(TERMS)):
            running = forward[row] * inverse[row]
            for inner in range(row + 1, TERMS):
                running = running - lower[inner, row] * solved[inner]
            solved[row] = running
        for row in range(TERMS):
            beta[row, band] = solved[row]
    return beta


def dot(a, b):
    return jnp.dot(a, b, preferred_element_type=f32)


def add_parts(total, size):
    return sum(total[i * size : (i + 1) * size] for i in range(total.shape[0] // size))


def dot_nt(a, b):
    return lax.dot_general(a, b, (((1,), (1,)), ((), ())), preferred_element_type=f32)


def one_hot(shape, first, second):
    row = lax.broadcasted_iota(jnp.int32, shape, 0)
    col = lax.broadcasted_iota(jnp.int32, shape, 1)
    return jnp.where(first(row) == second(col), 1.0, 0.0)


def design_of(infos, dates, parts):
    count = len(infos)
    total = count * dates * parts
    wide = -(-count * dates // LANES) * LANES
    shift = parts.bit_length() - 1
    low_bits = parts - 1
    lane = lax.broadcasted_iota(jnp.int32, (TERMS, LANES), 1)
    sums = [jnp.zeros((TERMS, wide), f32) for _ in range(3)]
    for n, info in enumerate(infos):
        info = info.astype(f32)
        top = info[0:TERMS]
        high = jnp.where(lane < 64, top, 0.0)
        low = jnp.where(lane < 64, pltpu.roll(top, 64, 1), 0.0)
        for c, part in enumerate((high, info[TERMS:], low)):
            if wide > LANES:
                part = jnp.concatenate([part, jnp.zeros((TERMS, wide - LANES), f32)], axis=1)
            if n:
                part = pltpu.roll(part, n * dates, 1)
            sums[c] = sums[c] + part
    x = sums[0] + sums[1] + sums[2]
    stacked = jnp.concatenate(sums + [jnp.zeros((TERMS, wide), f32)], axis=0).astype(bf16)
    spread = one_hot((total, wide), lambda t: t >> shift, lambda d: d).astype(bf16)
    size = TERMS * parts
    repeat = one_hot((3 * size, 4 * TERMS), lambda r: r >> shift, lambda c: c).astype(bf16)
    rows = dot(repeat, stacked)
    same = one_hot((3 * size, total), lambda r: r & low_bits, lambda t: t & low_bits)
    left = (dot_nt(rows.astype(bf16), spread) * same).astype(bf16)
    high, mid, low = rows[0:size], rows[size : 2 * size], rows[2 * size :]
    six = jnp.concatenate([high, mid, low, high, mid, high], axis=0).astype(bf16)
    same = one_hot((total, 6 * size), lambda t: t & low_bits, lambda r: r & low_bits)
    x_wide = (dot_nt(spread, six) * same).astype(bf16)
    products = jnp.concatenate(
        [x[i : i + 1] * x[i:] for i in range(TERMS)] + [jnp.zeros((4, wide), f32)], axis=0
    )
    padded = products.shape[0]
    used = len(pairs) * parts
    product_parts = jnp.concatenate(
        [part.astype(f32) for part in split3_kernel(products)], axis=0
    ).astype(bf16)
    gram_left = []
    same = one_hot((used, total), lambda r: r & low_bits, lambda t: t & low_bits)
    for c in range(3):
        repeat = one_hot((used, 3 * padded), lambda r: (r >> shift) + c * padded, lambda n: n)
        rows = dot(repeat.astype(bf16), product_parts)
        gram_left.append((dot_nt(rows.astype(bf16), spread) * same).astype(bf16))
    return left, gram_left, x_wide


def keep_design(infos, dates, parts, outs):
    left, gram_left, x_wide = design_of(infos, dates, parts)
    used = len(pairs) * parts
    outs[0][...] = left
    for c in range(3):
        outs[1][c * used : (c + 1) * used, :] = gram_left[c]
    outs[2][...] = x_wide


def absorb(blocks, bands, dates, parts, left_ref, gram_left_ref, y_ref, mask_ref):
    rows = dates * parts
    masks = []
    products = []
    for n, block in enumerate(blocks):
        here = slice(n * rows, (n + 1) * rows)
        mask = block[bands * rows : (bands + 1) * rows, :]
        mask_ref[here, :] = mask
        masks.append(mask)
        product = []
        for b in range(bands):
            y = block[b * rows : (b + 1) * rows, :]
            y_ref[here, b * LANES : (b + 1) * LANES] = y
            product.append(y * mask)
        products.append(jnp.concatenate(product, axis=1))
    product = jnp.concatenate(products, axis=0)
    cross_sum = add_parts(dot(left_ref[...], product), TERMS * parts)
    gram_sum = add_parts(dot(gram_left_ref[...], jnp.concatenate(masks, axis=0)), len(pairs) * parts)
    return cross_sum, gram_sum


def absorb_kernel(shape, early_count, late_count, *refs):
    bands, dates, parts = shape
    blocks, info_ref = refs[:early_count], refs[early_count]
    infos = [info_ref[n * INFO_ROWS : (n + 1) * INFO_ROWS, :] for n in range(late_count)]
    early, late, sums = refs[-10:-5], refs[-5:-2], refs[-2:]
    start = (bands + 1) * dates * parts
    keep_design([block[start:, :] for block in blocks], dates, parts, early[:3])
    keep_design(infos, dates, parts, late)
    sums[0][...], sums[1][...] = absorb(
        blocks, bands, dates, parts, early[0], early[1], early[3], early[4]
    )


def fit_and_spread(parts, bands, gram_sum, cross_sum, groups):
    gram = {ij: gram_sum[n * parts : (n + 1) * parts] for n, ij in enumerate(pairs)}
    cross = {
        (k, b): cross_sum[k * parts : (k + 1) * parts, b * LANES : (b + 1) * LANES]
        for k in range(TERMS)
        for b in range(bands)
    }
    beta = solve(gram, cross, bands)
    flat = jnp.concatenate(
        [jnp.concatenate([beta[k, b] for k in range(TERMS)], axis=0) for b in range(bands)], axis=1
    )
    high, mid, low = split3_kernel(flat)
    right = jnp.concatenate([high, high, high, mid, mid, low], axis=0)
    spread = jnp.zeros((8, LANES), f32)
    for y_ref, x_ref, power_ref, weight_of in groups:
        size = y_ref.shape[0]
        misfit = y_ref[...].astype(f32) - dot(x_ref[...], right)
        power = jnp.zeros((size, LANES), f32)
        for b in range(bands):
            part = misfit[:, b * LANES : (b + 1) * LANES]
            power = power + part * part
        if power_ref is not None:
            power_ref[...] = power
        weighted = weight_of() * power
        spread = spread + jnp.sum(weighted.reshape(size // 8, 8, LANES), axis=0)
    spread = add_parts(spread, parts)
    return beta, spread / (bands * (1.0 + gram[0, 0]))


def first_kernel(shape, late_count, *refs):
    bands, dates, parts = shape
    blocks = refs[:late_count]
    left_ref, gram_left_ref, x_ref = refs[late_count : late_count + 3]
    early_x, early_y, early_mask, early_cross, early_gram = refs[late_count + 3 : late_count + 8]
    y_ref, mask_ref, early_power, late_power, variance_ref = refs[late_count + 8 :]
    cross_sum, gram_sum = absorb(
        blocks, bands, dates, parts, left_ref, gram_left_ref, y_ref, mask_ref
    )
    groups = [
        (early_y, early_x, early_power, lambda: early_mask[...].astype(f32)),
        (y_ref, x_ref, late_power, lambda: mask_ref[...].astype(f32)),
    ]
    _, variance = fit_and_spread(
        parts, bands, gram_sum + early_gram[...], cross_sum + early_cross[...], groups
    )
    for place in range(variance_ref.shape[0]):
        variance_ref[place] = variance


def smoothed(field_ref, parts, width, rows, spaces, count):
    group = LANES // width
    space = lax.axis_index("space")
    me = lax.axis_index("date")

    def rows_of(space_now, date_now):
        block = field_ref[space_now * count + date_now]
        return [block if h == 0 else pltpu.roll(block, LANES - h * width, 1) for h in range(group)]

    lane = lax.broadcasted_iota(jnp.int32, (rows, LANES), 1)
    sums = []
    for ds in (-1, 0, 1):
        space_now = jnp.clip(space + ds, 0, spaces - 1)
        row_ok = jnp.where((space + ds >= 0) & (space + ds < spaces), 1.0, 0.0)
        across = jnp.zeros((rows, LANES), f32)
        for dd in (-1, 0, 1):
            date_now = jnp.clip(me + dd, 0, count - 1)
            ok = jnp.where((me + dd >= 0) & (me + dd < count), row_ok, 0.0)
            block = jnp.concatenate(rows_of(space_now, date_now), axis=0)
            block = jnp.where(lane < width, block, 0.0) * ok
            for offset in range(-2, 3):
                shift = dd * width - offset
                if abs(shift) >= width and dd * offset <= 0:
                    continue
                moved = block if shift == 0 else pltpu.roll(block, shift % LANES, 1)
                source = lane + offset - dd * width
                across = across + jnp.where((source >= 0) & (source < width), moved, 0.0)
        sums.append(across)
    tall = jnp.concatenate([sums[0][rows - 2 :], sums[1], sums[2][:2]], axis=0)
    total = tall[0:rows]
    for offset in range(1, 5):
        total = total + tall[offset : offset + rows]
    row_index = lax.broadcasted_iota(jnp.int32, (rows, LANES), 0) + space * rows
    col_index = lane + me * width

    def window(index, whole):
        return (jnp.minimum(index + 2, whole - 1) - jnp.maximum(index - 2, 0) + 1).astype(f32)

    smooth = total / (window(row_index, spaces * rows) * window(col_index, count * width))
    return smooth


def to_lanes(tall, parts, width):
    group = LANES // width
    lane = lax.broadcasted_iota(jnp.int32, (parts, LANES), 1)
    out = tall[0:parts]
    for h in range(1, group):
        moved = pltpu.roll(tall[h * parts : (h + 1) * parts], h * width, 1)
        out = jnp.where(lane >= h * width, moved, out)
    return out


def to_rows(block, width):
    group = LANES // width
    tall = [block if h == 0 else pltpu.roll(block, LANES - h * width, 1) for h in range(group)]
    return jnp.concatenate(tall, axis=0)[:, 0:width]


def second_kernel(shape, *refs):
    bands, parts, width, rows, spaces, count = shape
    field_ref = refs[0]
    groups = [refs[1:7], refs[7:13]]
    coefficient_ref, variance_ref = refs[13:15]
    weight_ref = refs[15]
    smooth = smoothed(field_ref, parts, width, rows, spaces, count)
    smooth = to_lanes(smooth, parts, width)
    scale = 1.0 / (bands * (TUKEY * TUKEY) * (smooth + EPS))
    scale = jnp.concatenate([scale] * (8 // parts), axis=0)
    early = groups[0][3].shape[0]
    cross_sum = gram_sum = 0.0
    for base, (left_ref, gram_left_ref, _, y_ref, mask_ref, power_ref) in zip((0, early), groups):
        size = y_ref.shape[0]
        power = power_ref[...].reshape(size // 8, 8, LANES)
        left_over = 1.0 - jnp.minimum(power * scale[None], 1.0)
        mask = mask_ref[...].astype(f32)
        weight = mask * (left_over * left_over).reshape(size, LANES)
        weight_ref[base : base + size, :] = weight
        wy_parts = [[], []]
        for b in range(bands):
            y = y_ref[:, b * LANES : (b + 1) * LANES].astype(f32)
            for n, part in enumerate(split2_kernel(weight * y)):
                wy_parts[n].append(part)
        wy_parts = [jnp.concatenate(part, axis=1) for part in wy_parts]

        def moments(a_ref, b_parts, used):
            total = add_parts(dot(a_ref[...], b_parts[0]), used)
            return total + add_parts(dot(a_ref[0 : 2 * used, :], b_parts[1]), used)

        gram_sum = gram_sum + moments(gram_left_ref, split2_kernel(weight), len(pairs) * parts)
        cross_sum = cross_sum + moments(left_ref, wy_parts, TERMS * parts)

    beta, variance = fit_and_spread(
        parts,
        bands,
        gram_sum,
        cross_sum,
        [
            (groups[0][3], groups[0][2], None, lambda: weight_ref[0:early, :]),
            (
                groups[1][3],
                groups[1][2],
                None,
                lambda: weight_ref[early:, :],
            ),
        ],
    )
    for place in range(variance_ref.shape[0]):
        variance_ref[place] = variance
    for b in range(bands):
        for k in range(TERMS):
            coefficient_ref[b, k] = to_rows(beta[k, b], width)


def last_kernel(shape, field_ref, noise_ref):
    bands, parts, width, rows, spaces, count = shape
    smooth = smoothed(field_ref, parts, width, rows, spaces, count)
    noise_ref[...] = jnp.sqrt(smooth[:, 0:width] + EPS)


def on_device(obs, valid, days):
    bands, dates, rows, cols = obs.shape
    count = lax.axis_size("date")
    spaces = lax.axis_size("space")
    me = lax.axis_index("date")
    width = cols // count
    group = LANES // width
    parts = rows // group
    half = count // 2
    quarter = half // 2
    early_count, late_count = half + quarter, quarter
    early_rows = early_count * dates * parts
    late_rows = late_count * dates * parts
    shape = (bands, parts, width, rows, spaces, count)
    vmem = pl.BlockSpec(memory_space=pltpu.VMEM)
    params = pltpu.CompilerParams(vmem_limit_bytes=VMEM_BYTES)

    blocks = packed_blocks(obs, valid, days, count, me, width)
    received = [blocks[0]] + [None] * (count - 1)

    def swap(k, after=None):
        block = blocks[k]
        if after is not None:
            block, received[after] = lax.optimization_barrier((block, received[after]))
        received[k] = lax.ppermute(block, "date", [(i, i ^ k) for i in range(count)])

    for k in range(half, count, 2):
        swap(k)
    for k in reversed(range(1, half)):
        swap(k)
    for k in range(half, count, 2):
        swap(k + 1, after=k ^ 2)

    infos = jnp.concatenate([block[-INFO_ROWS:] for block in received[half::2]], axis=0)
    infos = lax.ppermute(infos, "date", [(i, i ^ 1) for i in range(count)])
    early_blocks = [*received[:half], *received[half::2]]
    late_blocks = received[half + 1 :: 2]

    def design_shapes(total):
        return [
            jax.ShapeDtypeStruct((3 * TERMS * parts, total), bf16),
            jax.ShapeDtypeStruct((3 * len(pairs) * parts, total), bf16),
            jax.ShapeDtypeStruct((total, 6 * TERMS * parts), bf16),
        ]

    def data_shapes(total):
        return [
            jax.ShapeDtypeStruct((total, bands * LANES), bf16),
            jax.ShapeDtypeStruct((total, LANES), bf16),
        ]

    def power(total):
        return jax.ShapeDtypeStruct((total, LANES), f32)

    sums = [
        jax.ShapeDtypeStruct((TERMS * parts, bands * LANES), f32),
        jax.ShapeDtypeStruct((len(pairs) * parts, LANES), f32),
    ]
    send = jax.ShapeDtypeStruct((spaces * count, parts, LANES), f32)
    given = pl.pallas_call(
        functools.partial(absorb_kernel, (bands, dates, parts), early_count, late_count),
        out_shape=design_shapes(early_rows)
        + data_shapes(early_rows)
        + design_shapes(late_rows)
        + sums,
        in_specs=[vmem] * (early_count + 1),
        out_specs=[vmem] * 10,
        compiler_params=params,
        name="absorb",
    )(*early_blocks, infos)
    early, late, early_sums = given[:5], given[5:8], given[8:]
    *late_data, early_power, late_power, variance = pl.pallas_call(
        functools.partial(first_kernel, (bands, dates, parts), late_count),
        out_shape=data_shapes(late_rows) + [power(early_rows), power(late_rows), send],
        in_specs=[vmem] * (late_count + 8),
        out_specs=[vmem] * 5,
        compiler_params=params,
        name="first",
    )(*late_blocks, *late, *early[2:], *early_sums)
    late = [*late, *late_data]

    field = lax.all_to_all(variance, ("space", "date"), 0, 0, tiled=True)
    total = early_rows + late_rows
    coefficients, variance = pl.pallas_call(
        functools.partial(second_kernel, shape),
        out_shape=[jax.ShapeDtypeStruct((bands, TERMS, rows, width), f32), send],
        in_specs=[vmem] * 13,
        out_specs=[vmem] * 2,
        scratch_shapes=[pltpu.VMEM((total, LANES), f32)],
        compiler_params=params,
        name="second",
    )(field, *early, early_power, *late, late_power)
    field = lax.all_to_all(variance, ("space", "date"), 0, 0, tiled=True)
    noise = pl.pallas_call(
        functools.partial(last_kernel, shape),
        out_shape=jax.ShapeDtypeStruct((rows, width), f32),
        in_specs=[vmem],
        out_specs=vmem,
        compiler_params=params,
        name="last",
    )(field)
    return coefficients, noise


def solution(mesh):
    in_specs = (P(None, "date", "space", None), P("date", "space", None), P("date"))
    out_specs = (P(None, None, "space", "date"), P("space", "date"))
    return jax.shard_map(
        on_device, mesh=mesh, in_specs=in_specs, out_specs=out_specs, check_vma=False
    )
```
